128 devices in a mesh: sub: 16 (over x, y), grp: 8 (over z, core).
Axes of the slice: x: 4, y: 4, z: 4, core: 2. Of those that a mesh axis runs over, the one named last changes fastest.
Arguments:
- res_inner: bfloat16 [8192, 16, 144], P(('sub', 'grp')), may hold values from -6 to 6
- res_face: bfloat16 [16384, 16, 144], P(('sub', 'grp')), may hold values from -6 to 6
- inner_inv: bfloat16 [8192, 144, 144], P(('sub', 'grp')), may hold values from -0.5 to 0.5
- face_coupling: bfloat16 [16384, 144, 144], P(('sub', 'grp')), may hold values from -0.5 to 0.5
- face_elem: int32 [128, 128], P(('sub', 'grp')), may hold values from 0 to 63
- face_inv: bfloat16 [16384, 144, 144], P(('sub', 'grp')), may hold values from -0.5 to 0.5
- coarse_basis: bfloat16 [16384, 64, 144], P(('sub', 'grp')), may hold values from -0.0625 to 0.0625
- coarse_map: int32 [128, 64], P(('sub', 'grp')), may hold values from 0 to 2047
- coarse_inv: float32 [2048, 2048], P('grp'), as said below
- recv_index: int32 [128, 128], P(('sub', 'grp')), may hold values from 0 to 32, as said below
- sharers: int32 [128, 128], P(('sub', 'grp')), may hold values from 0 to 128, as said below
Outputs:
- inner_out: bfloat16 [8192, 16, 144], P(('sub', 'grp'))
- face_out: bfloat16 [16384, 16, 144], P(('sub', 'grp'))
The draws below stay inside these ranges and needn't reach their ends.
Inputs may be any that keep to these rules, and one draw needn't show every extreme that they name: `recv_index`: row o gives, for each subdomain s at position s, the index among the 32 blocks owned by subdomain o that slot o of subdomain s refers to, or 32 where that slot is unused. `sharers`: for a used slot, the number of used slots of all subdomains that refer to the same owned block, up to all 128 of them, which some block reaches; 0 exactly for unused slots. coarse_inv is symmetric.
All inputs are finite; a program needn't handle non-finite values.
Results may differ from the reference program's by a relative error of at most 0.006.
Values may be sent and summed in bfloat16 or wider, within the bound.
A program may use at most 128 MiB of HBM per device.

```python
import math
import jax
import jax.numpy as jnp
from jax import lax

B = 144
R = 16
E = 64
NC = 64
SUBS = 128
FACES = 128
OWNED = 32
NCG = 2048


def interface_tables(key):
    base = jax.random.fold_in(key, 5)
    key_load, key_roll, key_pick = jax.random.split(base, 3)
    count = SUBS
    load = jax.random.randint(key_load, (count,), 1, 5)
    roll = jax.random.randint(key_roll, (count, count), 0, 4)
    source = jnp.arange(count, dtype=jnp.int32)[:, None]
    target = jnp.arange(count, dtype=jnp.int32)[None, :]
    neighbour = target == (source + 1) % count
    live = roll < load[None, :]
    live = jnp.logical_or(live, target == 0)
    live = jnp.logical_or(live, neighbour)
    live = jnp.logical_or(live, target == source)
    picks = jax.random.randint(key_pick, (count, count), 0, OWNED)
    picks = jnp.where(jnp.logical_or(target == source, target == 0), 0, picks)
    index = jnp.where(live, picks, OWNED).astype(jnp.int32)
    owner_view = index.T
    levels = jnp.arange(OWNED + 1, dtype=jnp.int32)
    hits = jnp.sum((owner_view[:, :, None] == levels[None, None, :]).astype(jnp.int32), axis=1)
    owner_rows = jnp.broadcast_to(target, (count, count))
    shared = jnp.where(live, hits[owner_rows, index], 0).astype(jnp.int32)
    return (owner_view, shared)


def draw_recv_index(key, part):
    owner_view, shared = interface_tables(key)
    return owner_view


def draw_sharers(key, part):
    owner_view, shared = interface_tables(key)
    return shared


def draw_coarse_inv(key, part):
    base = jax.random.fold_in(key, 11)
    key_raw, key_diag = jax.random.split(base, 2)
    count = NCG
    raw = jax.random.normal(key_raw, (count, count), jnp.float32)
    symmetric = (raw + raw.T) * (0.35 / math.sqrt(count))
    diagonal = jnp.exp(jax.random.uniform(key_diag, (count,), jnp.float32, 0.0, 1.1))
    identity = jnp.eye(count, dtype=jnp.float32)
    full = symmetric + identity * diagonal[None, :]
    return full.astype(jnp.float32)


def set_ends(drawn, rng, smallest, high):
    shape = drawn.shape
    place = [jax.random.randint(jax.random.fold_in(rng, axis), (), 0, shape[axis]) for axis in range(len(shape))]
    drawn = drawn.at[tuple(place)].set(smallest)
    longest = shape.index(max(shape))
    place[longest] = (place[longest] + 1) % shape[longest]
    return drawn.at[tuple(place)].set(high)


def steps_of(rng, extent, shards, least, largest):
    def one(axis_at, blocks):
        draws = jax.random.uniform(jax.random.fold_in(jax.random.fold_in(rng, 6), axis_at), (blocks,), jnp.float32, least / len(shards), largest / len(shards))
        return jnp.repeat(jnp.exp(draws), extent[axis_at] // blocks).reshape((-1,) + (1,) * (len(extent) - axis_at - 1))

    loudness = one(*shards[0])
    for cut in shards[1:]:
        loudness = loudness * one(*cut)
    return loudness


def normal_values(own_key, shape, spread, bound, shards=(), kind=jnp.bfloat16):
    values = spread * jax.random.normal(own_key, shape, jnp.float32)
    if shards:
        values = values * steps_of(own_key, shape, shards, -0.22, 0.18)
    return jnp.clip(values, -bound, bound).astype(kind)


def setup_inputs(seed: int = 0) -> dict:
    key_of = jax.random.split(jax.random.key(seed), 12)
    return {
        "res_inner": normal_values(key_of[0], (SUBS * E, R, B), 1.0, 6.0, ((0, 128),)),
        "res_face": normal_values(key_of[1], (SUBS * FACES, R, B), 1.0, 6.0, ((0, 128),)),
        "inner_inv": normal_values(key_of[2], (SUBS * E, B, B), B ** -0.5, 0.5, ((0, 128),)),
        "face_coupling": normal_values(key_of[3], (SUBS * FACES, B, B), B ** -0.5, 0.5, ((0, 128),)),
        "face_elem": set_ends(jax.random.randint(key_of[4], (SUBS, FACES), 0, E), jax.random.fold_in(key_of[4], 1), 0, E - 1).astype(jnp.int32),
        "face_inv": normal_values(key_of[5], (SUBS * FACES, B, B), B ** -0.5, 0.5, ((0, 128),)),
        "coarse_basis": normal_values(key_of[6], (SUBS * FACES, NC, B), (B * NC) ** -0.5, 0.0625, ((0, 128),)),
        "coarse_map": set_ends(jax.random.randint(key_of[7], (SUBS, NC), 0, NCG), jax.random.fold_in(key_of[7], 1), 0, NCG - 1).astype(jnp.int32),
        "coarse_inv": draw_coarse_inv(jax.random.fold_in(key_of[11], 71), 0),
        "recv_index": draw_recv_index(jax.random.fold_in(key_of[11], 71), 0),
        "sharers": draw_sharers(jax.random.fold_in(key_of[11], 71), 0),
    }


def assemble(sent, recv_index):
    columns = jnp.swapaxes(sent, 0, 1)

    def per_owner(items):
        column, index = items
        summed = jax.ops.segment_sum(column.astype(jnp.float32), index, num_segments=OWNED + 1)[:OWNED].astype(jnp.bfloat16)
        padded = jnp.concatenate([summed, jnp.zeros((1,) + summed.shape[1:], jnp.bfloat16)], 0)
        return padded[index]

    returned = lax.map(per_owner, (columns, recv_index))
    return jnp.swapaxes(returned, 0, 1)


def reference(res_inner, res_face, inner_inv, face_coupling, face_elem, face_inv, coarse_basis, coarse_map, coarse_inv, recv_index, sharers):
    inner = res_inner.reshape(SUBS, E, R, B)
    faced = res_face.reshape(SUBS, FACES, R, B)
    inverse = inner_inv.reshape(SUBS, E, B, B)
    coupling = face_coupling.reshape(SUBS, FACES, B, B)
    local_inv = face_inv.reshape(SUBS, FACES, B, B)
    basis = coarse_basis.reshape(SUBS, FACES, NC, B)
    weights = jnp.where(sharers > 0, 1.0 / jnp.maximum(sharers, 1).astype(jnp.float32), 0.0).astype(jnp.float32)

    def condense(items):
        block, face, inv_block, couple, elems, weight = items
        inner_w = jnp.einsum('erb,ecb->erc', block.astype(jnp.float32), inv_block.astype(jnp.float32)).astype(jnp.bfloat16)
        nearby = inner_w[elems]
        condensed = face.astype(jnp.float32) - jnp.einsum('lrb,lcb->lrc', nearby.astype(jnp.float32), couple.astype(jnp.float32))
        return (weight[:, None, None] * condensed).astype(jnp.bfloat16)

    sent = lax.map(condense, (inner, faced, inverse, coupling, face_elem, weights))
    gathered = assemble(sent, recv_index)
    restricted = (weights[:, :, None, None] * gathered.astype(jnp.float32)).astype(jnp.bfloat16)

    def project(items):
        base, restr = items
        return jnp.einsum('ljb,lrb->jr', base.astype(jnp.float32), restr.astype(jnp.float32))

    local_coarse = lax.map(project, (basis, restricted))
    coarse_rhs = jax.ops.segment_sum(local_coarse.reshape(SUBS * NC, R), coarse_map.reshape(-1), num_segments=NCG)
    coarse_sol = jnp.dot(coarse_inv, coarse_rhs, precision=lax.Precision.HIGHEST)
    picked = coarse_sol[coarse_map].astype(jnp.bfloat16)

    def correct(items):
        base, pick, restr, inv_block, weight = items
        coarse_part = jnp.einsum('ljb,jr->lrb', base.astype(jnp.float32), pick.astype(jnp.float32))
        local_part = jnp.einsum('lrb,lcb->lrc', restr.astype(jnp.float32), inv_block.astype(jnp.float32))
        return (weight[:, None, None] * (coarse_part + local_part)).astype(jnp.bfloat16)

    weighted = lax.map(correct, (basis, picked, restricted, local_inv, weights))
    face_out = assemble(weighted, recv_index)

    def extend(items):
        block, face_val, couple, elems, inv_block = items
        contrib = jnp.einsum('lrc,lcb->lrb', face_val.astype(jnp.float32), couple.astype(jnp.float32))
        scattered = jax.ops.segment_sum(contrib, elems, num_segments=E)
        inner_rhs = (block.astype(jnp.float32) - scattered).astype(jnp.bfloat16)
        return jnp.einsum('erb,ecb->erc', inner_rhs.astype(jnp.float32), inv_block.astype(jnp.float32)).astype(jnp.bfloat16)

    inner_out = lax.map(extend, (inner, face_out, coupling, face_elem, inverse))
    return inner_out.reshape(SUBS * E, R, B), face_out.reshape(SUBS * FACES, R, B)
```

```python
import jax
import jax.numpy as jnp
from jax import lax
from jax.experimental import pallas as pl
from jax.experimental.pallas import tpu as pltpu
from jax.sharding import PartitionSpec as P

MESH = pl.DeviceIdType.MESH
N = 128
ROWS = 18
PITCH = 24


def place(t):
    return (t // 8, t % 8)


def assemble_kernel(x_ref, row_ref, col_ref, o_ref, recv, wide, wide2, back, ssem, rsem, lsem, ssem2, rsem2, lsem2):
    me = lax.axis_index("sub") * 8 + lax.axis_index("grp")
    barrier = pltpu.get_barrier_semaphore()

    def greet(i, c):
        pl.semaphore_signal(barrier, inc=1, device_id=place(lax.rem(me + i, N)), device_id_type=MESH)
        return c

    lax.fori_loop(1, N, greet, 0)
    pl.semaphore_wait(barrier, N - 1)

    def remote(src, dst, t, s, r):
        return pltpu.make_async_remote_copy(
            src_ref=src, dst_ref=dst, send_sem=s, recv_sem=r, device_id=place(t), device_id_type=MESH
        )

    def send(i, c):
        t = lax.rem(me + i, N)
        remote(x_ref.at[t], recv.at[me], t, ssem, rsem).start()
        return c

    own = pltpu.make_async_copy(x_ref.at[me], recv.at[me], lsem)
    own.start()
    lax.fori_loop(1, N, send, 0)
    own.wait()
    rest = pl.ds(0, N - 1)
    remote(x_ref.at[rest], recv.at[rest], 0, ssem, rsem).wait()

    def widen(s, c):
        wide[pl.ds(pl.multiple_of(s * PITCH, 8), ROWS)] = recv[s].astype(jnp.float32)
        return c

    lax.fori_loop(0, N, widen, 0)
    same = jnp.where((row_ref[...] == col_ref[...]) & (row_ref[...] < 32), 1.0, 0.0).astype(jnp.bfloat16)
    for k in range(ROWS):
        part = wide[pl.ds(k, N, stride=PITCH), :].astype(jnp.bfloat16)
        wide2[pl.ds(k, N, stride=PITCH), :] = jnp.dot(same, part, preferred_element_type=jnp.float32)

    def give(i, c):
        t = lax.rem(me + i, N)
        back[t] = wide2[pl.ds(pl.multiple_of(t * PITCH, 8), ROWS)].astype(jnp.bfloat16)
        remote(back.at[t], o_ref.at[me], t, ssem2, rsem2).start()
        return c

    back[me] = wide2[pl.ds(pl.multiple_of(me * PITCH, 8), ROWS)].astype(jnp.bfloat16)
    own = pltpu.make_async_copy(back.at[me], o_ref.at[me], lsem2)
    own.start()
    lax.fori_loop(1, N, give, 0)
    own.wait()
    remote(back.at[rest], o_ref.at[rest], 0, ssem2, rsem2).wait()


def assemble(x, index):
    vm = pl.BlockSpec(memory_space=pltpu.VMEM)
    packed = jax.ShapeDtypeStruct((N, ROWS, 128), jnp.bfloat16)
    out = pl.pallas_call(
        assemble_kernel,
        out_shape=packed,
        in_specs=[vm] * 3,
        out_specs=vm,
        scratch_shapes=[
            pltpu.VMEM((N, ROWS, 128), jnp.bfloat16),
            pltpu.VMEM((N * PITCH, 128), jnp.float32),
            pltpu.VMEM((N * PITCH, 128), jnp.float32),
            pltpu.VMEM((N, ROWS, 128), jnp.bfloat16),
        ]
        + [pltpu.SemaphoreType.DMA] * 6,
        name="assemble",
        compiler_params=pltpu.CompilerParams(
            collective_id=0, has_side_effects=True, vmem_limit_bytes=32 << 20
        ),
    )(x.reshape(N, ROWS, 128), index.reshape(1, N), index.reshape(N, 1))
    return out.reshape(x.shape)


def cut_along(x, dim, size):
    before, after = (x.shape[:dim], x.shape[dim + 1 :])
    return jnp.moveaxis(x.reshape(*before, size, -1, *after), dim, 0)


def sum_at_owner(x, axis, dim):
    size = lax.axis_size(axis)
    blocks = lax.all_to_all(cut_along(x, dim, size), axis, 0, 0, tiled=True)
    return jnp.sum(blocks, axis=0)


def copy_for_each(x, axis):
    size = lax.axis_size(axis)
    return lax.all_to_all(jnp.broadcast_to(x[None], (size, *x.shape)), axis, 0, 0, tiled=True)


def over_copies(x, axis):
    everything = copy_for_each(x, axis)
    return jnp.sum(everything, axis=0)


def body(
    res_inner,
    res_face,
    inner_inv,
    face_coupling,
    face_elem,
    face_inv,
    coarse_basis,
    coarse_map,
    coarse_inv,
    recv_index,
    sharers,
):
    num_faces = res_face.shape[0]
    elements = res_inner.shape[0]
    num_coarse = coarse_inv.shape[1]
    counts = sharers[0]
    weights = jnp.where(counts > 0, 1.0 / jnp.maximum(counts, 1).astype(jnp.float32), 0.0)
    inner_w = jnp.einsum(
        "erb,ecb->erc", res_inner, inner_inv, preferred_element_type=jnp.float32
    ).astype(jnp.bfloat16)
    pick_elem = (face_elem[0][:, None] == jnp.arange(elements, dtype=jnp.int32)[None, :]).astype(
        jnp.bfloat16
    )
    nearby = jnp.dot(
        pick_elem, inner_w.reshape(elements, -1), preferred_element_type=jnp.float32
    ).astype(jnp.bfloat16).reshape(res_face.shape)
    condensed = res_face.astype(jnp.float32) - jnp.einsum(
        "lrb,lcb->lrc", nearby, face_coupling, preferred_element_type=jnp.float32
    )
    sent = (weights[:, None, None] * condensed).astype(jnp.bfloat16)
    gathered = assemble(sent, recv_index[0])
    restricted = (weights[:, None, None] * gathered.astype(jnp.float32)).astype(jnp.bfloat16)
    local_coarse = jnp.einsum(
        "ljb,lrb->jr", coarse_basis, restricted, preferred_element_type=jnp.float32
    )
    coarse_onehot = (
        coarse_map[0][None, :] == jnp.arange(num_coarse, dtype=jnp.int32)[:, None]
    ).astype(jnp.float32)
    partial_rhs = jnp.dot(coarse_onehot, local_coarse, precision=lax.Precision.HIGHEST)
    share = sum_at_owner(partial_rhs, "grp", 0)
    rows_total = over_copies(share, "sub")
    column_term = lax.dot_general(
        coarse_inv, rows_total, (((0,), (0,)), ((), ())), precision=lax.Precision.HIGHEST
    )
    coarse_sol = over_copies(column_term, "grp")
    picked = jnp.einsum(
        "kj,kr->jr", coarse_onehot, coarse_sol, precision=lax.Precision.HIGHEST
    ).astype(jnp.bfloat16)
    coarse_part = jnp.einsum(
        "ljb,jr->lrb", coarse_basis, picked, preferred_element_type=jnp.float32
    )
    local_part = jnp.einsum(
        "lrb,lcb->lrc", restricted, face_inv, preferred_element_type=jnp.float32
    )
    weighted = (weights[:, None, None] * (coarse_part + local_part)).astype(jnp.bfloat16)
    face_out = assemble(weighted, recv_index[0])
    contrib = jnp.einsum(
        "lrc,lcb->lrb", face_out, face_coupling, preferred_element_type=jnp.float32
    )
    elem_onehot = (face_elem[0][None, :] == jnp.arange(elements, dtype=jnp.int32)[:, None]).astype(
        jnp.float32
    )
    scattered = jnp.dot(
        elem_onehot, contrib.reshape(num_faces, -1), precision=lax.Precision.HIGHEST
    ).reshape(res_inner.shape)
    inner_rhs = (res_inner.astype(jnp.float32) - scattered).astype(jnp.bfloat16)
    inner_out = jnp.einsum(
        "erb,ecb->erc", inner_rhs, inner_inv, preferred_element_type=jnp.float32
    ).astype(jnp.bfloat16)
    return (inner_out, face_out)


def solution(mesh):
    return jax.shard_map(
        body,
        mesh=mesh,
        in_specs=(
            P(("sub", "grp"), None, None),
            P(("sub", "grp"), None, None),
            P(("sub", "grp"), None, None),
            P(("sub", "grp"), None, None),
            P(("sub", "grp"), None),
            P(("sub", "grp"), None, None),
            P(("sub", "grp"), None, None),
            P(("sub", "grp"), None),
            P("grp", None),
            P(("sub", "grp"), None),
            P(("sub", "grp"), None),
        ),
        out_specs=(P(("sub", "grp"), None, None), P(("sub", "grp"), None, None)),
        check_vma=False,
    )
```

```python
import jax
import jax.numpy as jnp
from jax import lax
from jax.experimental import pallas as pl
from jax.experimental.pallas import tpu as pltpu
from jax.sharding import PartitionSpec as P

MESH = pl.DeviceIdType.MESH
N = 128
E = 64
R = 16
B = 144
NC = 64
NCG = 2048
GRP = 8
SUB = 16
SHARE = NCG // GRP
ROWS = 18
PITCH = 24
BF = jnp.bfloat16
F32 = jnp.float32


def place(t):
    return (t // GRP, t % GRP)


def remote(src, dst, device, s, r):
    return pltpu.make_async_remote_copy(
        src_ref=src, dst_ref=dst, send_sem=s, recv_sem=r, device_id=device, device_id_type=MESH
    )


def own_group():
    row = lax.broadcasted_iota(jnp.int32, (R, 128), 0)
    lane = lax.broadcasted_iota(jnp.int32, (R, 128), 1)
    return (row % 8) == (lane // 16)


def pack(out, t, value):
    out[t, 0:R, :] = value[:, 0:128].astype(BF)
    tail = jnp.where(own_group(), jnp.concatenate([value[:, 128:B]] * 8, axis=1), 0.0)
    out[t, R:ROWS, :] = jnp.sum(tail.reshape(2, 8, 128), axis=1).astype(BF)


def unpack(ref, t):
    tail = ref[t, R:ROWS, :].astype(F32)
    tail = jnp.broadcast_to(tail[:, None, :], (2, 8, 128)).reshape(R, 128)
    tail = jnp.where(own_group(), tail, 0.0)
    for shift in (64, 32, 16):
        tail = tail + pltpu.roll(tail, shift, 1)
    return jnp.concatenate([ref[t, 0:R, :].astype(F32), tail[:, 0:16]], axis=1)


def pieces(x):
    high = x.astype(BF)
    rest = x - high.astype(F32)
    mid = rest.astype(BF)
    low = (rest - mid.astype(F32)).astype(BF)
    return jnp.concatenate([high, mid, low], axis=0)


def gather3(x):
    return x[0:R] + x[R : 2 * R] + x[2 * R : 3 * R]


def rows_times(a, b):
    return lax.dot_general(a, b, (((1,), (1,)), ((), ())), preferred_element_type=F32)


def main_kernel(
    res_inner_h, res_face_h, inner_inv_h, coupling_h, face_inv_h, basis_h, coarse_inv_h,
    map_block, map_col, index_row, index_col, elem, weight,
    result, coupling_out,
    res_inner, inner_inv, inner_w, res_face, face_rows, stage, coupling, face_inv, basis_stage, basis,
    coarse_inv, coarse_high, coarse_low, pick, own_pick, maps,
    sent, received, wide, wide2, back, gathered, restricted, local,
    part, part_in, share, share_in, chosen, chosen_in,
    load_sems, send_sems, recv_sems, own_sems,
):
    sub = lax.axis_index("sub")
    grp = lax.axis_index("grp")
    me = sub * GRP + grp
    barrier = pltpu.get_barrier_semaphore()

    def load(src, dst, k):
        return pltpu.make_async_copy(src, dst, load_sems.at[k])

    load(res_inner_h, res_inner, 0).start()
    load(inner_inv_h, inner_inv, 1).start()
    load(coupling_h, stage, 2).start()
    load(res_face_h, res_face, 3).start()
    load(basis_h, basis_stage, 4).start()
    load(coarse_inv_h, coarse_inv, 5).start()

    def greet(i):
        pl.semaphore_signal(barrier, inc=1, device_id=place(lax.rem(me + i, N)), device_id_type=MESH)

    def inner(e, c):
        inner_w[e] = rows_times(res_inner[e], inner_inv[e]).astype(BF)
        return c

    def inner_greet(e, c):
        greet(2 * e)
        greet(2 * e + 1)
        return inner(e, c)

    load(res_inner_h, res_inner, 0).wait()
    load(inner_inv_h, inner_inv, 1).wait()
    greet(1)
    inner(0, 0)
    lax.fori_loop(1, E, inner_greet, 0, unroll=3)

    def turn(src, dst, q):
        part_rows = src[pl.ds(pl.multiple_of(q * 16, 16), 16)]
        part_rows = jnp.swapaxes(jnp.swapaxes(part_rows, 1, 2), 0, 1)
        dst[:, pl.ds(pl.multiple_of(q * 16, 16), 16), :] = part_rows

    def turns(src, dst, first, last):
        def one(q, c):
            turn(src, dst, q)
            return c

        lax.fori_loop(first, last, one, 0)

    load(res_face_h, res_face, 3).wait()
    turns(res_face, face_rows, 0, 1)
    load(coupling_h, stage, 2).wait()
    turns(stage, coupling, 0, 9)
    load(face_inv_h, stage, 6).start()
    save = load(coupling, coupling_out, 7)
    save.start()

    pl.semaphore_wait(barrier, N - 1)

    def map_copy(i):
        return remote(map_block, maps.at[grp], (sub, lax.rem(grp + i, GRP)), send_sems.at[0], recv_sems.at[0])

    def each(first, last, f, unroll=1):
        def one(i, c):
            f(i)
            return c

        lax.fori_loop(first, last, one, 0, unroll=unroll)

    own_map = pltpu.make_async_copy(map_block, maps.at[grp], own_sems.at[0])
    own_map.start()
    each(1, GRP, lambda i: map_copy(i).start())

    def exchange(source, target, k, fill, unroll):
        fill(me)
        own = pltpu.make_async_copy(source.at[me], target.at[me], own_sems.at[k])
        own.start()

        def one(i):
            t = lax.rem(me + i, N)
            fill(t)
            remote(source.at[t], target.at[me], place(t), send_sems.at[k], recv_sems.at[k]).start()

        each(1, N, one, unroll)
        return own

    def arrive(source, target, k, own):
        own.wait()
        rest = pl.ds(0, N - 1)
        remote(source.at[rest], target.at[rest], (sub, grp), send_sems.at[k], recv_sems.at[k]).wait()

    def condense(t):
        product = rows_times(inner_w[elem[t]], coupling[t])
        pack(sent.at[0], t, weight[t] * (face_rows[t].astype(F32) - product))

    own = exchange(sent.at[0], received.at[0], 1, condense, 4)
    load(face_inv_h, stage, 6).wait()
    turns(stage, face_inv, 0, 4)
    arrive(sent.at[0], received.at[0], 1, own)

    same = jnp.where((index_row[...] == index_col[...]) & (index_row[...] < 32), 1.0, 0.0).astype(BF)

    def owner_sum(source):
        def widen(s):
            wide[pl.ds(pl.multiple_of(s * PITCH, 8), ROWS)] = source[s].astype(F32)

        each(0, N, widen, 4)
        for k in range(ROWS):
            rows = wide[pl.ds(k, N, stride=PITCH), :].astype(BF)
            wide2[pl.ds(k, N, stride=PITCH), :] = jnp.dot(same, rows, preferred_element_type=F32)

    def narrow(target):
        def one(t):
            target[t] = wide2[pl.ds(pl.multiple_of(t * PITCH, 8), ROWS)].astype(BF)

        return one

    owner_sum(received.at[0])
    own = exchange(back.at[0], gathered, 2, narrow(back.at[0]), 4)

    turns(stage, face_inv, 4, 9)
    load(basis_h, basis_stage, 4).wait()
    turns(basis_stage, basis, 0, 4)
    load(coarse_inv_h, coarse_inv, 5).wait()

    def split(q):
        rows = pl.ds(pl.multiple_of(q * 16, 16), 16)
        high = coarse_inv[rows, :].astype(BF)
        coarse_high[rows, :] = high
        coarse_low[rows, :] = (coarse_inv[rows, :] - high.astype(F32)).astype(BF)

    each(0, SHARE // 16, split)
    own_map.wait()
    seven = pl.ds(0, GRP - 1)
    remote(maps.at[seven], maps.at[seven], (sub, grp), send_sems.at[0], recv_sems.at[0]).wait()
    map_row = jnp.concatenate([maps[g, 0:1, 0:NC] for g in range(GRP)], axis=1)

    def mark(q):
        at = lax.broadcasted_iota(jnp.int32, (128, GRP * NC), 0) + q * 128
        pick[pl.ds(pl.multiple_of(q * 128, 128), 128), :] = jnp.where(map_row == at, 1.0, 0.0).astype(BF)

    each(0, NCG // 128, mark)
    at = lax.broadcasted_iota(jnp.int32, (NC, NCG), 1)
    own_pick[...] = jnp.where(map_col[...] == at, 1.0, 0.0).astype(BF)

    arrive(back.at[0], gathered, 2, own)

    def project(t, total):
        rows = (weight[t] * unpack(gathered, t)).astype(BF)
        restricted[t] = rows
        return total + rows_times(rows, basis[t])

    local_coarse = lax.fori_loop(0, N, project, jnp.zeros((R, NC), F32), unroll=4)

    partial = gather3(jnp.dot(pieces(local_coarse), own_pick[...], preferred_element_type=F32))
    for g in range(GRP):
        part[g] = partial[:, g * SHARE : (g + 1) * SHARE]

    own = pltpu.make_async_copy(part.at[grp], part_in.at[grp], own_sems.at[3])
    own.start()

    def ring_send(source, target, k):
        def one(i):
            t = lax.rem(grp + i, GRP)
            remote(source.at[t], target.at[grp], (sub, t), send_sems.at[k], recv_sems.at[k]).start()

        each(1, GRP, one)

    def ring_wait(source, target, k):
        remote(source.at[seven], target.at[seven], (sub, grp), send_sems.at[k], recv_sems.at[k]).wait()

    def solve_local(t):
        local[t] = rows_times(restricted[t], face_inv[t])

    ring_send(part, part_in, 3)
    each(0, 48, solve_local, 4)
    own.wait()
    ring_wait(part, part_in, 3)
    share[...] = jnp.sum(part_in[...], axis=0)
    own = pltpu.make_async_copy(share, share_in.at[sub], own_sems.at[4])
    own.start()

    def share_copy(i):
        t = lax.rem(sub + i, SUB)
        remote(share, share_in.at[sub], (t, grp), send_sems.at[4], recv_sems.at[4]).start()

    each(1, SUB, share_copy)
    each(48, N, solve_local, 4)
    own.wait()
    fifteen = pl.ds(0, SUB - 1)
    remote(share_in.at[fifteen], share_in.at[fifteen], (sub, grp), send_sems.at[4], recv_sems.at[4]).wait()
    total = pieces(jnp.sum(share_in[...], axis=0))
    term = gather3(
        jnp.dot(total, coarse_high[...], preferred_element_type=F32)
        + jnp.dot(total, coarse_low[...], preferred_element_type=F32)
    )
    picked = gather3(jnp.dot(pieces(term), pick[...], preferred_element_type=F32))
    for g in range(GRP):
        chosen[g, :, 0:NC] = picked[:, g * NC : (g + 1) * NC]
        chosen[g, :, NC:128] = jnp.zeros((R, 128 - NC), F32)
    own = pltpu.make_async_copy(chosen.at[grp], chosen_in.at[grp], own_sems.at[5])
    own.start()
    ring_send(chosen, chosen_in, 5)
    own.wait()
    ring_wait(chosen, chosen_in, 5)
    mine = jnp.sum(chosen_in[...], axis=0)[:, 0:NC].astype(BF)

    def correct(t):
        value = local[t] + jnp.dot(mine, basis[t], preferred_element_type=F32)
        pack(sent.at[1], t, weight[t] * value)

    own = exchange(sent.at[1], received.at[1], 6, correct, 4)
    arrive(sent.at[1], received.at[1], 6, own)
    owner_sum(received.at[1])
    own = exchange(back.at[1], result, 7, narrow(back.at[1]), 4)
    arrive(back.at[1], result, 7, own)
    save.wait()


def extend_kernel(elem, face, coupling, res_inner, inner_inv, inner_out, face_out, rows, total):
    step = pl.program_id(0)
    steps = pl.num_programs(0)

    @pl.when(step == 0)
    def _():
        total[...] = res_inner[...].astype(F32)

    def one(i, c):
        t = step * 16 + i
        value = unpack(face, t).astype(BF)
        rows[t] = value
        e = elem[t]
        total[e] = total[e] - jnp.dot(value, coupling[i], preferred_element_type=F32)
        return c

    lax.fori_loop(0, 16, one, 0, unroll=4)

    @pl.when(step == steps - 1)
    def _():
        def inner(e, c):
            inner_out[e] = rows_times(total[e].astype(BF), inner_inv[e]).astype(BF)
            return c

        lax.fori_loop(0, E, inner, 0, unroll=4)

        def turn(q, c):
            part = rows[pl.ds(pl.multiple_of(q * 128, 128), 128)]
            face_out[...] = jnp.swapaxes(jnp.swapaxes(part, 0, 1), 1, 2)
            return c

        lax.fori_loop(0, 1, turn, 0)


def body(
    res_inner, res_face, inner_inv, face_coupling, face_elem, face_inv, coarse_basis, coarse_map, coarse_inv,
    recv_index, sharers,
):
    counts = sharers[0]
    weight = jnp.where(counts > 0, 1.0 / jnp.maximum(counts, 1).astype(F32), 0.0)
    index = recv_index[0]
    elem = face_elem[0]
    vm = pl.BlockSpec(memory_space=pltpu.VMEM)
    hbm = pl.BlockSpec(memory_space=pl.ANY)
    sm = pl.BlockSpec(memory_space=pltpu.SMEM)
    slots_last = (1, 2, 0)
    packed = (N, ROWS, 128)
    map_block = jnp.broadcast_to(jnp.pad(coarse_map, ((0, 0), (0, 128 - NC))), (8, 128))
    result, coupling = pl.pallas_call(
        main_kernel,
        out_shape=(jax.ShapeDtypeStruct(packed, BF), jax.ShapeDtypeStruct((N, B, B), BF)),
        in_specs=[hbm] * 7 + [vm] * 4 + [sm] * 2,
        out_specs=(vm, hbm),
        scratch_shapes=[
            pltpu.VMEM((E, R, B), BF),
            pltpu.VMEM((E, B, B), BF),
            pltpu.VMEM((E, R, B), BF),
            pltpu.VMEM((R, B, N), BF),
            pltpu.VMEM((N, R, B), BF),
            pltpu.VMEM((B, B, N), BF),
            pltpu.VMEM((N, B, B), BF),
            pltpu.VMEM((N, B, B), BF),
            pltpu.VMEM((NC, B, N), BF),
            pltpu.VMEM((N, NC, B), BF),
            pltpu.VMEM((SHARE, NCG), F32),
            pltpu.VMEM((SHARE, NCG), BF),
            pltpu.VMEM((SHARE, NCG), BF),
            pltpu.VMEM((NCG, GRP * NC), BF),
            pltpu.VMEM((NC, NCG), BF),
            pltpu.VMEM((GRP, 8, 128), jnp.int32),
            pltpu.VMEM((2, *packed), BF),
            pltpu.VMEM((2, *packed), BF),
            pltpu.VMEM((N * PITCH, 128), F32),
            pltpu.VMEM((N * PITCH, 128), F32),
            pltpu.VMEM((2, *packed), BF),
            pltpu.VMEM(packed, BF),
            pltpu.VMEM((N, R, B), BF),
            pltpu.VMEM((N, R, B), F32),
            pltpu.VMEM((GRP, R, SHARE), F32),
            pltpu.VMEM((GRP, R, SHARE), F32),
            pltpu.VMEM((R, SHARE), F32),
            pltpu.VMEM((SUB, R, SHARE), F32),
            pltpu.VMEM((GRP, R, 128), F32),
            pltpu.VMEM((GRP, R, 128), F32),
            pltpu.SemaphoreType.DMA((8,)),
            pltpu.SemaphoreType.DMA((8,)),
            pltpu.SemaphoreType.DMA((8,)),
            pltpu.SemaphoreType.DMA((8,)),
        ],
        name="assemble_all",
        compiler_params=pltpu.CompilerParams(
            collective_id=0, has_side_effects=True, vmem_limit_bytes=61 << 20
        ),
    )(
        res_inner,
        jnp.transpose(res_face, slots_last),
        inner_inv,
        jnp.transpose(face_coupling, slots_last),
        jnp.transpose(face_inv, slots_last),
        jnp.transpose(coarse_basis, slots_last),
        coarse_inv,
        map_block,
        coarse_map.reshape(NC, 1),
        index.reshape(1, N),
        index.reshape(N, 1),
        elem,
        weight,
    )
    whole = lambda i: (0, 0, 0)
    inner_out, face_out = pl.pallas_call(
        extend_kernel,
        grid=(N // 16,),
        out_shape=(jax.ShapeDtypeStruct((E, R, B), BF), jax.ShapeDtypeStruct((R, B, N), BF)),
        in_specs=[
            sm,
            pl.BlockSpec(packed, whole),
            pl.BlockSpec((16, B, B), lambda i: (i, 0, 0)),
            pl.BlockSpec((E, R, B), whole),
            pl.BlockSpec((E, B, B), whole),
        ],
        out_specs=(pl.BlockSpec((E, R, B), whole), pl.BlockSpec((R, B, N), whole)),
        scratch_shapes=[pltpu.VMEM((N, R, B), BF), pltpu.VMEM((E, R, B), F32)],
        name="extend",
        compiler_params=pltpu.CompilerParams(vmem_limit_bytes=40 << 20),
    )(elem, result, coupling, res_inner, inner_inv)
    return inner_out, jnp.transpose(face_out, (2, 0, 1))


def solution(mesh):
    split = P(("sub", "grp"), None, None)
    table = P(("sub", "grp"), None)
    return jax.shard_map(
        body,
        mesh=mesh,
        in_specs=(
            split, split, split, split, table, split, split, table, P("grp", None), table, table,
        ),
        out_specs=(split, split),
        check_vma=False,
    )
```

```python
import jax
import jax.numpy as jnp
from jax import lax
from jax.experimental import pallas as pl
from jax.experimental.pallas import tpu as pltpu
from jax.sharding import PartitionSpec as P

MESH = pl.DeviceIdType.MESH
N = 128
E = 64
R = 16
B = 144
NC = 64
NCG = 2048
GRP = 8
SUB = 16
SHARE = NCG // GRP
ROWS = 18
PITCH = 24
BF = jnp.bfloat16
F32 = jnp.float32


def place(t):
    return (t // GRP, t % GRP)


def remote(src, dst, device, s, r):
    return pltpu.make_async_remote_copy(
        src_ref=src, dst_ref=dst, send_sem=s, recv_sem=r, device_id=device, device_id_type=MESH
    )


def pack(out, t, value):
    out[t, 0:R, :] = value[:, 0:128].astype(BF)
    row = lax.broadcasted_iota(jnp.int32, (R, 128), 0)
    lane = lax.broadcasted_iota(jnp.int32, (R, 128), 1)
    tail = jnp.concatenate([value[:, 128:B], jnp.zeros((R, 112), F32)], axis=1)
    for shift in (16, 32, 64):
        tail = tail + pltpu.roll(tail, shift, 1)
    tail = jnp.where((row + lane // 16) % 8 == 0, tail, 0.0)
    out[t, R:ROWS, :] = jnp.sum(tail.reshape(2, 8, 128), axis=1).astype(BF)


def unpack(ref, t):
    tail = ref[t, R:ROWS, :].astype(F32)
    tail = jnp.broadcast_to(tail[:, None, :], (2, 8, 128)).reshape(R, 128)
    tail = pltpu.roll(tail, 0, 1, stride=16, stride_axis=0)
    return jnp.concatenate([ref[t, 0:R, :].astype(F32), tail[:, 0:16]], axis=1)


def pieces(x):
    high = x.astype(BF)
    rest = x - high.astype(F32)
    mid = rest.astype(BF)
    low = (rest - mid.astype(F32)).astype(BF)
    return jnp.concatenate([high, mid, low], axis=0)


def gather3(x):
    return x[0:R] + x[R : 2 * R] + x[2 * R : 3 * R]


def rows_times(a, b):
    return lax.dot_general(a, b, (((1,), (1,)), ((), ())), preferred_element_type=F32)


def main_kernel(
    res_inner_h, res_face_h, inner_inv_h, coupling_h, face_inv_h, basis_h, coarse_inv_h,
    map_row_own, index_row, sharers, elem,
    result, coupling_out,
    res_inner, inner_inv, inner_w, res_face, face_rows, stage, coupling, face_inv, basis_stage, basis,
    coarse_inv, coarse_high, coarse_low, pick, own_pick, maps,
    sent, received, wide, wide2, back, gathered, restricted, local,
    part, part_in, share, share_in, chosen, chosen_in, map_block, weight, contrast,
    entered, load_sems, send_sems, recv_sems, own_sems,
):
    sub = lax.axis_index("sub")
    grp = lax.axis_index("grp")
    me = sub * GRP + grp
    barrier = pltpu.get_barrier_semaphore()

    def load(src, dst, k):
        return pltpu.make_async_copy(src, dst, load_sems.at[k])

    load(res_inner_h, res_inner, 0).start()
    load(inner_inv_h, inner_inv, 1).start()

    def signal(semaphore, device):
        pl.semaphore_signal(semaphore, inc=1, device_id=device, device_id_type=MESH)

    def each(first, last, f, unroll=1):
        def one(i, c):
            f(i)
            return c

        lax.fori_loop(first, last, one, 0, unroll=unroll)

    each(1, GRP, lambda i: signal(barrier, (sub, lax.rem(grp + i, GRP))))
    each(1, SUB, lambda i: signal(barrier, (lax.rem(sub + i, SUB), grp)))

    def tall(row):
        return jnp.broadcast_to(row, (N, N)).T

    counts = sharers[...]
    weight[...] = tall(jnp.where(counts > 0, 1.0 / jnp.maximum(counts, 1).astype(F32), 0.0))
    map_own = jnp.concatenate([map_row_own[...], jnp.zeros((1, 128 - NC), jnp.int32)], axis=1)
    map_block[...] = jnp.broadcast_to(map_own, (8, 128))
    index = index_row[...].astype(F32)
    contrast[...] = jnp.where((index == tall(index)) & (index < 32.0), 1.0, 0.0).astype(BF)

    def inner(e):
        inner_w[e] = rows_times(res_inner[e], inner_inv[e]).astype(BF)

    load(res_inner_h, res_inner, 0).wait()
    load(inner_inv_h, inner_inv, 1).wait()
    load(res_face_h, res_face, 3).start()
    load(coupling_h, stage, 2).start()
    each(0, E, inner, 8)
    pl.semaphore_wait(barrier, GRP + SUB - 2)
    each(1, SUB, lambda i: signal(entered, (lax.rem(sub + i, SUB), grp)))

    def turn(src, dst, q):
        part_rows = src[pl.ds(pl.multiple_of(q * 16, 16), 16)]
        part_rows = jnp.swapaxes(jnp.swapaxes(part_rows, 1, 2), 0, 1)
        dst[:, pl.ds(pl.multiple_of(q * 16, 16), 16), :] = part_rows

    def turns(src, dst, first, last):
        def one(q, c):
            turn(src, dst, q)
            return c

        lax.fori_loop(first, last, one, 0)

    load(res_face_h, res_face, 3).wait()
    turns(res_face, face_rows, 0, 1)
    load(coupling_h, stage, 2).wait()
    turns(stage, coupling, 0, 9)
    load(face_inv_h, stage, 6).start()
    load(basis_h, basis_stage, 4).start()
    load(coarse_inv_h, coarse_inv, 5).start()
    save = load(coupling, coupling_out, 7)
    save.start()

    pl.semaphore_wait(entered, SUB - 1)

    def map_copy(i):
        return remote(map_block, maps.at[grp], (sub, lax.rem(grp + i, GRP)), send_sems.at[0], recv_sems.at[0])

    own_map = pltpu.make_async_copy(map_block, maps.at[grp], own_sems.at[0])
    own_map.start()
    each(1, GRP, lambda i: map_copy(i).start())

    def quad(i):
        return lax.rem(me // 4 + i, N // 4) * 4

    def exchange(source, target, k, fill):
        def give(t):
            remote(source.at[t], target.at[me], place(t), send_sems.at[k], recv_sems.at[k]).start()

        def batch(q):
            for i in range(4):
                fill(quad(q * 4 + i))

        batch(0)
        own = pltpu.make_async_copy(source.at[me], target.at[me], own_sems.at[k])
        own.start()
        each(1, 4, lambda j: give(quad(0) + lax.rem(me + j, 4)))
        each(4, 16, lambda j: give(quad(j // 4) + lax.rem(me + j, 4)))

        def more(q):
            batch(q)
            each(16 * q, 16 * q + 16, lambda j: give(quad(j // 4) + lax.rem(me + j, 4)))

        each(1, N // 16, more)
        return own

    def arrive(source, target, k, own):
        own.wait()
        rest = pl.ds(0, N - 1)
        remote(source.at[rest], target.at[rest], (sub, grp), send_sems.at[k], recv_sems.at[k]).wait()

    def scaled(t, value):
        scale = jnp.broadcast_to(weight[pl.ds(t, 1), :], (R, 128))
        return jnp.concatenate([scale, scale[:, 0:16]], axis=1) * value

    def condense(base):
        for t in [base + k for k in range(4)]:
            product = rows_times(inner_w[elem[0, t]], coupling[t])
            pack(sent.at[0], t, scaled(t, face_rows[t].astype(F32) - product))

    own = exchange(sent.at[0], received.at[0], 1, condense)
    load(face_inv_h, stage, 6).wait()
    turns(stage, face_inv, 0, 4)
    arrive(sent.at[0], received.at[0], 1, own)

    same = contrast[...]

    def owner_sum(source):
        def widen(s):
            wide[pl.ds(pl.multiple_of(s * PITCH, 8), ROWS)] = source[s].astype(F32)

        each(0, N, widen, 8)
        for k in range(ROWS):
            rows = wide[pl.ds(k, N, stride=PITCH), :].astype(BF)
            wide2[pl.ds(k, N, stride=PITCH), :] = jnp.dot(same, rows, preferred_element_type=F32)

    def narrow(target):
        def one(base):
            for t in [base + k for k in range(4)]:
                target[t] = wide2[pl.ds(pl.multiple_of(t * PITCH, 8), ROWS)].astype(BF)

        return one

    owner_sum(received.at[0])
    own = exchange(back.at[0], gathered, 2, narrow(back.at[0]))

    turns(stage, face_inv, 4, 9)
    load(basis_h, basis_stage, 4).wait()
    turns(basis_stage, basis, 0, 4)
    load(coarse_inv_h, coarse_inv, 5).wait()

    def split(q):
        rows = pl.ds(pl.multiple_of(q * 16, 16), 16)
        high = coarse_inv[rows, :].astype(BF)
        coarse_high[rows, :] = high
        coarse_low[rows, :] = (coarse_inv[rows, :] - high.astype(F32)).astype(BF)

    each(0, SHARE // 16, split)
    own_map.wait()
    seven = pl.ds(0, GRP - 1)
    remote(maps.at[seven], maps.at[seven], (sub, grp), send_sems.at[0], recv_sems.at[0]).wait()
    map_row = jnp.concatenate([maps[g, 0:1, 0:NC] for g in range(GRP)], axis=1)

    def mark(q):
        at = lax.broadcasted_iota(jnp.int32, (128, GRP * NC), 0) + q * 128
        pick[pl.ds(pl.multiple_of(q * 128, 128), 128), :] = jnp.where(map_row == at, 1.0, 0.0).astype(BF)

    each(0, NCG // 128, mark)
    map_tall = tall(map_own.astype(F32))[0:NC]
    for q in range(NCG // 128):
        at = (lax.broadcasted_iota(jnp.int32, (NC, 128), 1) + q * 128).astype(F32)
        own_pick[:, q * 128 : (q + 1) * 128] = jnp.where(map_tall == at, 1.0, 0.0).astype(BF)

    arrive(back.at[0], gathered, 2, own)

    def basis4(q):
        return basis[pl.ds(pl.multiple_of(q * 4, 4), 4)].reshape(4 * NC, B)

    def project(q, total):
        rows = []
        for t in [4 * q + k for k in range(4)]:
            rows.append(scaled(t, unpack(gathered, t)).astype(BF))
            restricted[t] = rows[-1]
        return total + rows_times(jnp.concatenate(rows, axis=0), basis4(q))

    crossed = lax.fori_loop(0, N // 4, project, jnp.zeros((4 * R, 4 * NC), F32), unroll=2)
    local_coarse = sum(crossed[k * R : (k + 1) * R, k * NC : (k + 1) * NC] for k in range(4))

    partial = gather3(jnp.dot(pieces(local_coarse), own_pick[...], preferred_element_type=F32))
    for g in range(GRP):
        part[g] = partial[:, g * SHARE : (g + 1) * SHARE]

    own = pltpu.make_async_copy(part.at[grp], part_in.at[grp], own_sems.at[3])
    own.start()

    def ring_send(source, target, k):
        def one(i):
            t = lax.rem(grp + i, GRP)
            remote(source.at[t], target.at[grp], (sub, t), send_sems.at[k], recv_sems.at[k]).start()

        each(1, GRP, one)

    def ring_wait(source, target, k):
        remote(source.at[seven], target.at[seven], (sub, grp), send_sems.at[k], recv_sems.at[k]).wait()

    def solve_local(t):
        local[t] = rows_times(restricted[t], face_inv[t])

    ring_send(part, part_in, 3)
    each(0, 64, solve_local, 8)
    own.wait()
    ring_wait(part, part_in, 3)
    share[...] = jnp.sum(part_in[...], axis=0)
    own = pltpu.make_async_copy(share, share_in.at[sub], own_sems.at[4])
    own.start()

    def share_copy(i):
        t = lax.rem(sub + i, SUB)
        remote(share, share_in.at[sub], (t, grp), send_sems.at[4], recv_sems.at[4]).start()

    each(1, SUB, share_copy)
    each(64, N, solve_local, 8)
    own.wait()
    fifteen = pl.ds(0, SUB - 1)
    remote(share_in.at[fifteen], share_in.at[fifteen], (sub, grp), send_sems.at[4], recv_sems.at[4]).wait()
    total = pieces(jnp.sum(share_in[...], axis=0))
    term = gather3(
        jnp.dot(total, coarse_high[...], preferred_element_type=F32)
        + jnp.dot(total, coarse_low[...], preferred_element_type=F32)
    )
    picked = gather3(jnp.dot(pieces(term), pick[...], preferred_element_type=F32))
    for g in range(GRP):
        chosen[g, :, 0:NC] = picked[:, g * NC : (g + 1) * NC]
        chosen[g, :, NC:128] = jnp.zeros((R, 128 - NC), F32)
    own = pltpu.make_async_copy(chosen.at[grp], chosen_in.at[grp], own_sems.at[5])
    own.start()
    ring_send(chosen, chosen_in, 5)
    own.wait()
    ring_wait(chosen, chosen_in, 5)
    mine = jnp.sum(chosen_in[...], axis=0)[:, 0:NC]
    row = lax.broadcasted_iota(jnp.int32, (4 * R, 4 * NC), 0) // R
    lane = lax.broadcasted_iota(jnp.int32, (4 * R, 4 * NC), 1) // NC
    mine4 = jnp.concatenate([jnp.concatenate([mine] * 4, axis=1)] * 4, axis=0)
    mine4 = jnp.where(row == lane, mine4, 0.0).astype(BF)

    def correct(base):
        coarse = jnp.dot(mine4, basis4(base // 4), preferred_element_type=F32)
        for k in range(4):
            pack(sent.at[1], base + k, scaled(base + k, local[base + k] + coarse[k * R : (k + 1) * R]))

    own = exchange(sent.at[1], received.at[1], 6, correct)
    arrive(sent.at[1], received.at[1], 6, own)
    owner_sum(received.at[1])
    own = exchange(back.at[1], result, 7, narrow(back.at[1]))
    arrive(back.at[1], result, 7, own)
    save.wait()


def extend_kernel(elem, face, coupling, res_inner_h, inner_inv_h, inner_out, face_out, rows, total, terms, res_inner, inner_inv, sems):
    step = pl.program_id(0)
    steps = pl.num_programs(0)
    first = pltpu.make_async_copy(res_inner_h, res_inner, sems.at[0])
    second = pltpu.make_async_copy(inner_inv_h, inner_inv, sems.at[1])

    @pl.when(step == 0)
    def _():
        first.start()
        second.start()

    def one(i, c):
        value = unpack(face, step * 16 + i).astype(BF)
        rows[step * 16 + i] = value
        terms[i] = jnp.dot(value, coupling[i], preferred_element_type=F32)
        return c

    lax.fori_loop(0, 16, one, 0, unroll=16)

    @pl.when(step == 0)
    def _():
        first.wait()
        total[...] = res_inner[...].astype(F32)

    def add(i, c):
        e = elem[0, step * 16 + i]
        total[e] = total[e] - terms[i]
        return c

    lax.fori_loop(0, 16, add, 0, unroll=4)

    @pl.when(step == steps - 1)
    def _():
        second.wait()

        def inner(e, c):
            inner_out[e] = rows_times(total[e].astype(BF), inner_inv[e]).astype(BF)
            return c

        lax.fori_loop(0, E, inner, 0, unroll=8)
        face_out[...] = jnp.swapaxes(jnp.swapaxes(rows[...], 0, 1), 1, 2)


def body(
    res_inner, res_face, inner_inv, face_coupling, face_elem, face_inv, coarse_basis, coarse_map, coarse_inv,
    recv_index, sharers,
):
    vm = pl.BlockSpec(memory_space=pltpu.VMEM)
    hbm = pl.BlockSpec(memory_space=pl.ANY)
    sm = pl.BlockSpec(memory_space=pltpu.SMEM)
    slots_last = (1, 2, 0)
    packed = (N, ROWS, 128)
    result, coupling = pl.pallas_call(
        main_kernel,
        out_shape=(jax.ShapeDtypeStruct(packed, BF), jax.ShapeDtypeStruct((N, B, B), BF)),
        in_specs=[hbm] * 7 + [vm] * 3 + [sm],
        out_specs=(vm, hbm),
        scratch_shapes=[
            pltpu.VMEM((E, R, B), BF),
            pltpu.VMEM((E, B, B), BF),
            pltpu.VMEM((E, R, B), BF),
            pltpu.VMEM((R, B, N), BF),
            pltpu.VMEM((N, R, B), BF),
            pltpu.VMEM((B, B, N), BF),
            pltpu.VMEM((N, B, B), BF),
            pltpu.VMEM((N, B, B), BF),
            pltpu.VMEM((NC, B, N), BF),
            pltpu.VMEM((N, NC, B), BF),
            pltpu.VMEM((SHARE, NCG), F32),
            pltpu.VMEM((SHARE, NCG), BF),
            pltpu.VMEM((SHARE, NCG), BF),
            pltpu.VMEM((NCG, GRP * NC), BF),
            pltpu.VMEM((NC, NCG), BF),
            pltpu.VMEM((GRP, 8, 128), jnp.int32),
            pltpu.VMEM((2, *packed), BF),
            pltpu.VMEM((2, *packed), BF),
            pltpu.VMEM((N * PITCH, 128), F32),
            pltpu.VMEM((N * PITCH, 128), F32),
            pltpu.VMEM((2, *packed), BF),
            pltpu.VMEM(packed, BF),
            pltpu.VMEM((N, R, B), BF),
            pltpu.VMEM((N, R, B), F32),
            pltpu.VMEM((GRP, R, SHARE), F32),
            pltpu.VMEM((GRP, R, SHARE), F32),
            pltpu.VMEM((R, SHARE), F32),
            pltpu.VMEM((SUB, R, SHARE), F32),
            pltpu.VMEM((GRP, R, 128), F32),
            pltpu.VMEM((GRP, R, 128), F32),
            pltpu.VMEM((8, 128), jnp.int32),
            pltpu.VMEM((N, N), F32),
            pltpu.VMEM((N, N), BF),
            pltpu.SemaphoreType.REGULAR,
            pltpu.SemaphoreType.DMA((8,)),
            pltpu.SemaphoreType.DMA((8,)),
            pltpu.SemaphoreType.DMA((8,)),
            pltpu.SemaphoreType.DMA((8,)),
        ],
        name="assemble_all",
        compiler_params=pltpu.CompilerParams(
            collective_id=0, has_side_effects=True, vmem_limit_bytes=61 << 20
        ),
    )(
        res_inner,
        jnp.transpose(res_face, slots_last),
        inner_inv,
        jnp.transpose(face_coupling, slots_last),
        jnp.transpose(face_inv, slots_last),
        jnp.transpose(coarse_basis, slots_last),
        coarse_inv,
        coarse_map,
        recv_index,
        sharers,
        face_elem,
    )
    whole = lambda i: (0, 0, 0)
    inner_out, face_out = pl.pallas_call(
        extend_kernel,
        grid=(N // 16,),
        out_shape=(jax.ShapeDtypeStruct((E, R, B), BF), jax.ShapeDtypeStruct((R, B, N), BF)),
        in_specs=[
            sm,
            pl.BlockSpec(packed, whole),
            pl.BlockSpec((16, B, B), lambda i: (i, 0, 0)),
            hbm,
            hbm,
        ],
        out_specs=(pl.BlockSpec((E, R, B), whole), pl.BlockSpec((R, B, N), whole)),
        scratch_shapes=[
            pltpu.VMEM((N, R, B), BF),
            pltpu.VMEM((E, R, B), F32),
            pltpu.VMEM((16, R, B), F32),
            pltpu.VMEM((E, R, B), BF),
            pltpu.VMEM((E, B, B), BF),
            pltpu.SemaphoreType.DMA((2,)),
        ],
        name="extend",
        compiler_params=pltpu.CompilerParams(vmem_limit_bytes=60 << 20),
    )(face_elem, result, coupling, res_inner, inner_inv)
    return inner_out, jnp.transpose(face_out, (2, 0, 1))


def solution(mesh):
    split = P(("sub", "grp"), None, None)
    table = P(("sub", "grp"), None)
    return jax.shard_map(
        body,
        mesh=mesh,
        in_specs=(
            split, split, split, split, table, split, split, table, P("grp", None), table, table,
        ),
        out_specs=(split, split),
        check_vma=False,
    )
```

```python
import jax
import jax.numpy as jnp
from jax import lax
from jax.experimental import pallas as pl
from jax.experimental.pallas import tpu as pltpu
from jax.sharding import PartitionSpec as P

MESH = pl.DeviceIdType.MESH
N = 128
E = 64
R = 16
B = 144
NC = 64
NCG = 2048
GRP = 8
SUB = 16
SHARE = NCG // GRP
ROWS = 18
PITCH = 24
BF = jnp.bfloat16
F32 = jnp.float32


def place(t):
    return (t // GRP, t % GRP)


def remote(src, dst, device, s, r):
    return pltpu.make_async_remote_copy(
        src_ref=src, dst_ref=dst, send_sem=s, recv_sem=r, device_id=device, device_id_type=MESH
    )


def pack(out, t, value):
    out[t, 0:R, :] = value[:, 0:128].astype(BF)
    row = lax.broadcasted_iota(jnp.int32, (R, 128), 0)
    lane = lax.broadcasted_iota(jnp.int32, (R, 128), 1)
    tail = jnp.concatenate([value[:, 128:B], jnp.zeros((R, 112), F32)], axis=1)
    for shift in (16, 32, 64):
        tail = tail + pltpu.roll(tail, shift, 1)
    tail = jnp.where((row + lane // 16) % 8 == 0, tail, 0.0)
    out[t, R:ROWS, :] = jnp.sum(tail.reshape(2, 8, 128), axis=1).astype(BF)


def unpack(ref, t):
    tail = ref[t, R:ROWS, :].astype(F32)
    tail = jnp.broadcast_to(tail[:, None, :], (2, 8, 128)).reshape(R, 128)
    tail = pltpu.roll(tail, 0, 1, stride=16, stride_axis=0)
    return jnp.concatenate([ref[t, 0:R, :].astype(F32), tail[:, 0:16]], axis=1)


def pieces(x):
    high = x.astype(BF)
    rest = x - high.astype(F32)
    mid = rest.astype(BF)
    low = (rest - mid.astype(F32)).astype(BF)
    return jnp.concatenate([high, mid, low], axis=0)


def gather3(x):
    return x[0:R] + x[R : 2 * R] + x[2 * R : 3 * R]


def rows_times(a, b):
    return lax.dot_general(a, b, (((1,), (1,)), ((), ())), preferred_element_type=F32)


def main_kernel(
    res_inner_h, res_face_h, inner_inv_h, coupling_h, face_inv_h, basis_h, coarse_inv_h,
    map_row_own, index_row, sharers, elem,
    rows_out, terms_out,
    res_inner, inner_inv, inner_w, res_face, face_rows, stage, coupling, face_inv, basis_stage, basis,
    coarse_inv, coarse_high, coarse_low, pick, own_pick, maps,
    sent, received, wide, wide2, back, gathered, gathered2, restricted, local,
    part, part_in, share, share_in, chosen, chosen_in, map_block, weight, contrast,
    entered, piece_sems, batch_sems, load_sems, send_sems, recv_sems, own_sems,
):
    sub = lax.axis_index("sub")
    grp = lax.axis_index("grp")
    me = sub * GRP + grp
    barrier = pltpu.get_barrier_semaphore()

    def load(src, dst, k):
        return pltpu.make_async_copy(src, dst, load_sems.at[k])

    load(res_inner_h, res_inner, 0).start()

    def piece(src, dst, q, k):
        rows = pl.ds(pl.multiple_of(q * 16, 16), 16)
        return pltpu.make_async_copy(src.at[rows], dst.at[rows], piece_sems.at[k + q])

    def inverse_piece(q):
        return piece(inner_inv_h, inner_inv, q, 0)

    def coupling_piece(q):
        return piece(coupling_h, stage, q, 4)

    for q in range(4):
        inverse_piece(q).start()
    load(res_face_h, res_face, 3).start()
    for q in range(9):
        coupling_piece(q).start()

    def signal(semaphore, device):
        pl.semaphore_signal(semaphore, inc=1, device_id=device, device_id_type=MESH)

    def each(first, last, f, unroll=1):
        def one(i, c):
            f(i)
            return c

        lax.fori_loop(first, last, one, 0, unroll=unroll)

    each(1, GRP, lambda i: signal(barrier, (sub, lax.rem(grp + i, GRP))))
    each(1, SUB, lambda i: signal(barrier, (lax.rem(sub + i, SUB), grp)))

    def tall(row):
        return jnp.broadcast_to(row, (N, N)).T

    counts = sharers[...]
    weight[...] = tall(jnp.where(counts > 0, 1.0 / jnp.maximum(counts, 1).astype(F32), 0.0))
    map_own = jnp.concatenate([map_row_own[...], jnp.zeros((1, 128 - NC), jnp.int32)], axis=1)
    map_block[...] = jnp.broadcast_to(map_own, (8, 128))
    index = index_row[...].astype(F32)
    contrast[...] = jnp.where((index == tall(index)) & (index < 32.0), 1.0, 0.0).astype(BF)

    def inner(e):
        inner_w[e] = rows_times(res_inner[e], inner_inv[e]).astype(BF)

    load(res_inner_h, res_inner, 0).wait()

    def inners(q):
        inverse_piece(q).wait()
        for e in range(16):
            inner(16 * q + e)

    each(0, 4, inners)
    pl.semaphore_wait(barrier, GRP + SUB - 2)
    each(1, SUB, lambda i: signal(entered, (lax.rem(sub + i, SUB), grp)))

    def turn(src, dst, q):
        part_rows = src[pl.ds(pl.multiple_of(q * 16, 16), 16)]
        part_rows = jnp.swapaxes(jnp.swapaxes(part_rows, 1, 2), 0, 1)
        dst[:, pl.ds(pl.multiple_of(q * 16, 16), 16), :] = part_rows

    def turns(src, dst, first, last):
        def one(q, c):
            turn(src, dst, q)
            return c

        lax.fori_loop(first, last, one, 0)

    load(res_face_h, res_face, 3).wait()
    turns(res_face, face_rows, 0, 1)

    def coupling_turn(q):
        coupling_piece(q).wait()
        turn(stage, coupling, q)

    each(0, 9, coupling_turn)
    load(face_inv_h, stage, 6).start()
    load(basis_h, basis_stage, 4).start()
    load(coarse_inv_h, coarse_inv, 5).start()

    pl.semaphore_wait(entered, SUB - 1)

    def map_copy(i):
        return remote(map_block, maps.at[grp], (sub, lax.rem(grp + i, GRP)), send_sems.at[0], recv_sems.at[0])

    own_map = pltpu.make_async_copy(map_block, maps.at[grp], own_sems.at[0])
    own_map.start()
    each(1, GRP, lambda i: map_copy(i).start())

    def quad(i):
        return lax.rem(me // 4 + i, N // 4) * 4

    def exchange(source, target, k, fill, arrived):
        def give(t, q):
            remote(source.at[t], target.at[me], place(t), send_sems.at[k], arrived(q)).start()

        def batch(q):
            for i in range(4):
                fill(quad(q * 4 + i))

        batch(0)
        own = pltpu.make_async_copy(source.at[me], target.at[me], own_sems.at[k])
        own.start()
        each(1, 4, lambda j: give(quad(0) + lax.rem(me + j, 4), 0))
        each(4, 16, lambda j: give(quad(j // 4) + lax.rem(me + j, 4), 0))

        def more(q):
            batch(q)
            each(16 * q, 16 * q + 16, lambda j: give(quad(j // 4) + lax.rem(me + j, 4), q))

        each(1, N // 16, more)
        return own

    def all_at_once(k):
        return lambda q: recv_sems.at[k]

    def in_batches(c):
        return lambda q: batch_sems.at[c * 8 + q]

    def sent_all(source, k):
        rest = source.at[pl.ds(0, N - 1)]
        remote(rest, rest, (sub, grp), send_sems.at[k], recv_sems.at[k]).wait_send()

    def arrive(source, target, k, own):
        own.wait()
        rest = target.at[pl.ds(0, N - 1)]
        remote(rest, rest, (sub, grp), send_sems.at[k], recv_sems.at[k]).wait_recv()
        sent_all(source, k)

    def arrive_in_batches(source, target, k, own, arrived, use, carry):
        def wait(q, count):
            some = target.at[pl.ds(0, count)]
            remote(some, some, (sub, grp), send_sems.at[k], arrived(q)).wait_recv()

        def use_batch(q, carry):
            return use([quad(N // 4 - 4 * q - i) for i in range(4)], carry)

        def next_batch(q, carry):
            wait(q, 16)
            return use_batch(q, carry)

        own.wait()
        wait(0, 15)
        carry = lax.fori_loop(1, N // 16, next_batch, use_batch(0, carry))
        sent_all(source, k)
        return carry

    def scaled(t, value):
        scale = jnp.broadcast_to(weight[pl.ds(t, 1), :], (R, 128))
        return jnp.concatenate([scale, scale[:, 0:16]], axis=1) * value

    def condense(base):
        for t in [base + k for k in range(4)]:
            product = rows_times(inner_w[elem[0, t]], coupling[t])
            pack(sent, t, scaled(t, face_rows[t].astype(F32) - product))

    own = exchange(sent, received.at[0], 1, condense, all_at_once(1))
    load(face_inv_h, stage, 6).wait()
    turns(stage, face_inv, 0, 4)
    arrive(sent, received.at[0], 1, own)

    same = contrast[...]

    def owner_sum(source):
        def widen(s):
            wide[pl.ds(pl.multiple_of(s * PITCH, 8), ROWS)] = source[s].astype(F32)

        each(0, N, widen, 8)
        for k in range(ROWS):
            rows = wide[pl.ds(k, N, stride=PITCH), :].astype(BF)
            wide2[pl.ds(k, N, stride=PITCH), :] = jnp.dot(same, rows, preferred_element_type=F32)

    def narrow(target):
        def one(base):
            for t in [base + k for k in range(4)]:
                target[t] = wide2[pl.ds(pl.multiple_of(t * PITCH, 8), ROWS)].astype(BF)

        return one

    owner_sum(received.at[0])
    own = exchange(back, gathered, 2, narrow(back), in_batches(0))

    turns(stage, face_inv, 4, 9)
    load(basis_h, basis_stage, 4).wait()
    turns(basis_stage, basis, 0, 4)
    load(coarse_inv_h, coarse_inv, 5).wait()

    def split(q):
        rows = pl.ds(pl.multiple_of(q * 16, 16), 16)
        high = coarse_inv[rows, :].astype(BF)
        coarse_high[rows, :] = high
        coarse_low[rows, :] = (coarse_inv[rows, :] - high.astype(F32)).astype(BF)

    each(0, SHARE // 16, split)
    own_map.wait()
    seven = pl.ds(0, GRP - 1)
    remote(maps.at[seven], maps.at[seven], (sub, grp), send_sems.at[0], recv_sems.at[0]).wait()
    map_row = jnp.concatenate([maps[g, 0:1, 0:NC] for g in range(GRP)], axis=1)

    def mark(q):
        at = lax.broadcasted_iota(jnp.int32, (128, GRP * NC), 0) + q * 128
        pick[pl.ds(pl.multiple_of(q * 128, 128), 128), :] = jnp.where(map_row == at, 1.0, 0.0).astype(BF)

    each(0, NCG // 128, mark)
    map_tall = tall(map_own.astype(F32))[0:NC]
    for q in range(NCG // 128):
        at = (lax.broadcasted_iota(jnp.int32, (NC, 128), 1) + q * 128).astype(F32)
        own_pick[:, q * 128 : (q + 1) * 128] = jnp.where(map_tall == at, 1.0, 0.0).astype(BF)

    def basis4(q):
        return basis[pl.ds(pl.multiple_of(q * 4, 4), 4)].reshape(4 * NC, B)

    def project(bases, total):
        for base in bases:
            rows = []
            for t in [base + k for k in range(4)]:
                rows.append(scaled(t, unpack(gathered, t)).astype(BF))
                restricted[t] = rows[-1]
            total = total + rows_times(jnp.concatenate(rows, axis=0), basis4(base // 4))
        return total

    crossed = arrive_in_batches(
        back, gathered, 2, own, in_batches(0), project, jnp.zeros((4 * R, 4 * NC), F32)
    )
    local_coarse = sum(crossed[k * R : (k + 1) * R, k * NC : (k + 1) * NC] for k in range(4))

    partial = gather3(jnp.dot(pieces(local_coarse), own_pick[...], preferred_element_type=F32))
    for g in range(GRP):
        part[g] = partial[:, g * SHARE : (g + 1) * SHARE]

    own = pltpu.make_async_copy(part.at[grp], part_in.at[grp], own_sems.at[3])
    own.start()

    def ring_send(source, target, k):
        def one(i):
            t = lax.rem(grp + i, GRP)
            remote(source.at[t], target.at[grp], (sub, t), send_sems.at[k], recv_sems.at[k]).start()

        each(1, GRP, one)

    def ring_wait(source, target, k):
        remote(source.at[seven], target.at[seven], (sub, grp), send_sems.at[k], recv_sems.at[k]).wait()

    def solve_local(t):
        local[t] = rows_times(restricted[t], face_inv[t])

    ring_send(part, part_in, 3)
    each(0, 64, solve_local, 8)
    own.wait()
    ring_wait(part, part_in, 3)
    share[...] = jnp.sum(part_in[...], axis=0)
    own = pltpu.make_async_copy(share, share_in.at[sub], own_sems.at[4])
    own.start()

    def share_copy(i):
        t = lax.rem(sub + i, SUB)
        remote(share, share_in.at[sub], (t, grp), send_sems.at[4], recv_sems.at[4]).start()

    each(1, SUB, share_copy)
    each(64, N, solve_local, 8)
    own.wait()
    fifteen = pl.ds(0, SUB - 1)
    remote(share_in.at[fifteen], share_in.at[fifteen], (sub, grp), send_sems.at[4], recv_sems.at[4]).wait()
    total = pieces(jnp.sum(share_in[...], axis=0))
    term = gather3(
        jnp.dot(total, coarse_high[...], preferred_element_type=F32)
        + jnp.dot(total, coarse_low[...], preferred_element_type=F32)
    )
    picked = gather3(jnp.dot(pieces(term), pick[...], preferred_element_type=F32))
    for g in range(GRP):
        chosen[g, :, 0:NC] = picked[:, g * NC : (g + 1) * NC]
        chosen[g, :, NC:128] = jnp.zeros((R, 128 - NC), F32)
    own = pltpu.make_async_copy(chosen.at[grp], chosen_in.at[grp], own_sems.at[5])
    own.start()
    ring_send(chosen, chosen_in, 5)
    own.wait()
    ring_wait(chosen, chosen_in, 5)
    mine = jnp.sum(chosen_in[...], axis=0)[:, 0:NC]
    row = lax.broadcasted_iota(jnp.int32, (4 * R, 4 * NC), 0) // R
    lane = lax.broadcasted_iota(jnp.int32, (4 * R, 4 * NC), 1) // NC
    mine4 = jnp.concatenate([jnp.concatenate([mine] * 4, axis=1)] * 4, axis=0)
    mine4 = jnp.where(row == lane, mine4, 0.0).astype(BF)

    def correct(base):
        coarse = jnp.dot(mine4, basis4(base // 4), preferred_element_type=F32)
        for k in range(4):
            pack(sent, base + k, scaled(base + k, local[base + k] + coarse[k * R : (k + 1) * R]))

    own = exchange(sent, received.at[1], 6, correct, all_at_once(6))
    arrive(sent, received.at[1], 6, own)
    owner_sum(received.at[1])
    own = exchange(back, gathered2, 7, narrow(back), in_batches(1))

    def extend(bases, carry):
        for base in bases:
            for t in [base + k for k in range(4)]:
                rows = unpack(gathered2, t).astype(BF)
                rows_out[t] = rows
                terms_out[t] = jnp.dot(rows, coupling[t], preferred_element_type=F32)
        return carry

    arrive_in_batches(back, gathered2, 7, own, in_batches(1), extend, 0)


def extend_kernel(
    elem, rows_h, terms_h, res_inner_h, inner_inv_h, inner_out, face_out,
    rows, terms, res_inner, total, inner_inv, sems,
):
    pairs = ((res_inner_h, res_inner), (terms_h, terms), (rows_h, rows), (inner_inv_h, inner_inv))
    loads = [pltpu.make_async_copy(src, dst, sems.at[k]) for k, (src, dst) in enumerate(pairs)]
    for one in loads:
        one.start()
    loads[0].wait()
    total[...] = res_inner[...].astype(F32)
    loads[1].wait()

    def add(t, c):
        e = elem[0, t]
        total[e] = total[e] - terms[t]
        return c

    lax.fori_loop(0, N, add, 0, unroll=8)
    loads[2].wait()
    face_out[...] = jnp.swapaxes(jnp.swapaxes(rows[...], 0, 1), 1, 2)
    loads[3].wait()

    def inner(e, c):
        inner_out[e] = rows_times(total[e].astype(BF), inner_inv[e]).astype(BF)
        return c

    lax.fori_loop(0, E, inner, 0, unroll=16)


def body(
    res_inner, res_face, inner_inv, face_coupling, face_elem, face_inv, coarse_basis, coarse_map, coarse_inv,
    recv_index, sharers,
):
    vm = pl.BlockSpec(memory_space=pltpu.VMEM)
    hbm = pl.BlockSpec(memory_space=pl.ANY)
    sm = pl.BlockSpec(memory_space=pltpu.SMEM)
    slots_last = (1, 2, 0)
    packed = (N, ROWS, 128)
    rows, terms = pl.pallas_call(
        main_kernel,
        out_shape=(jax.ShapeDtypeStruct((N, R, B), BF), jax.ShapeDtypeStruct((N, R, B), F32)),
        in_specs=[hbm] * 7 + [vm] * 3 + [sm],
        out_specs=(vm, vm),
        scratch_shapes=[
            pltpu.VMEM((E, R, B), BF),
            pltpu.VMEM((E, B, B), BF),
            pltpu.VMEM((E, R, B), BF),
            pltpu.VMEM((R, B, N), BF),
            pltpu.VMEM((N, R, B), BF),
            pltpu.VMEM((B, B, N), BF),
            pltpu.VMEM((N, B, B), BF),
            pltpu.VMEM((N, B, B), BF),
            pltpu.VMEM((NC, B, N), BF),
            pltpu.VMEM((N, NC, B), BF),
            pltpu.VMEM((SHARE, NCG), F32),
            pltpu.VMEM((SHARE, NCG), BF),
            pltpu.VMEM((SHARE, NCG), BF),
            pltpu.VMEM((NCG, GRP * NC), BF),
            pltpu.VMEM((NC, NCG), BF),
            pltpu.VMEM((GRP, 8, 128), jnp.int32),
            pltpu.VMEM(packed, BF),
            pltpu.VMEM((2, *packed), BF),
            pltpu.VMEM((N * PITCH, 128), F32),
            pltpu.VMEM((N * PITCH, 128), F32),
            pltpu.VMEM(packed, BF),
            pltpu.VMEM(packed, BF),
            pltpu.VMEM(packed, BF),
            pltpu.VMEM((N, R, B), BF),
            pltpu.VMEM((N, R, B), F32),
            pltpu.VMEM((GRP, R, SHARE), F32),
            pltpu.VMEM((GRP, R, SHARE), F32),
            pltpu.VMEM((R, SHARE), F32),
            pltpu.VMEM((SUB, R, SHARE), F32),
            pltpu.VMEM((GRP, R, 128), F32),
            pltpu.VMEM((GRP, R, 128), F32),
            pltpu.VMEM((8, 128), jnp.int32),
            pltpu.VMEM((N, N), F32),
            pltpu.VMEM((N, N), BF),
            pltpu.SemaphoreType.REGULAR,
            pltpu.SemaphoreType.DMA((16,)),
            pltpu.SemaphoreType.DMA((16,)),
            pltpu.SemaphoreType.DMA((8,)),
            pltpu.SemaphoreType.DMA((8,)),
            pltpu.SemaphoreType.DMA((8,)),
            pltpu.SemaphoreType.DMA((8,)),
        ],
        name="assemble_all",
        compiler_params=pltpu.CompilerParams(
            collective_id=0, has_side_effects=True, vmem_limit_bytes=61 << 20
        ),
    )(
        res_inner,
        jnp.transpose(res_face, slots_last),
        inner_inv,
        jnp.transpose(face_coupling, slots_last),
        jnp.transpose(face_inv, slots_last),
        jnp.transpose(coarse_basis, slots_last),
        coarse_inv,
        coarse_map,
        recv_index,
        sharers,
        face_elem,
    )
    inner_out, face_out = pl.pallas_call(
        extend_kernel,
        out_shape=(jax.ShapeDtypeStruct((E, R, B), BF), jax.ShapeDtypeStruct((R, B, N), BF)),
        in_specs=[sm, hbm, hbm, hbm, hbm],
        out_specs=(vm, vm),
        scratch_shapes=[
            pltpu.VMEM((N, R, B), BF),
            pltpu.VMEM((N, R, B), F32),
            pltpu.VMEM((E, R, B), BF),
            pltpu.VMEM((E, R, B), F32),
            pltpu.VMEM((E, B, B), BF),
            pltpu.SemaphoreType.DMA((4,)),
        ],
        name="extend",
        compiler_params=pltpu.CompilerParams(vmem_limit_bytes=61 << 20),
    )(face_elem, rows, terms, res_inner, inner_inv)
    return inner_out, jnp.transpose(face_out, (2, 0, 1))


def solution(mesh):
    split = P(("sub", "grp"), None, None)
    table = P(("sub", "grp"), None)
    return jax.shard_map(
        body,
        mesh=mesh,
        in_specs=(
            split, split, split, split, table, split, split, table, P("grp", None), table, table,
        ),
        out_specs=(split, split),
        check_vma=False,
    )
```

```python
import jax
import jax.numpy as jnp
from jax import lax
from jax.experimental import pallas as pl
from jax.experimental.pallas import tpu as pltpu
from jax.sharding import PartitionSpec as P

MESH = pl.DeviceIdType.MESH
N = 128
E = 64
R = 16
B = 144
NC = 64
NCG = 2048
GRP = 8
SUB = 16
SHARE = NCG // GRP
ROWS = 18
PITCH = 24
BF = jnp.bfloat16
F32 = jnp.float32


def place(t):
    return (t // GRP, t % GRP)


def remote(src, dst, device, s, r):
    return pltpu.make_async_remote_copy(
        src_ref=src, dst_ref=dst, send_sem=s, recv_sem=r, device_id=device, device_id_type=MESH
    )


def put(out, t, rows):
    out[t] = rows.reshape(ROWS // 2, 2, 128).astype(BF)


def get(ref, t):
    return ref[t].reshape(ROWS, 128).astype(F32)


def pack(out, t, value):
    row = lax.broadcasted_iota(jnp.int32, (R, 128), 0)
    lane = lax.broadcasted_iota(jnp.int32, (R, 128), 1)
    tail = jnp.concatenate([value[:, 128:B], jnp.zeros((R, 112), F32)], axis=1)
    for shift in (16, 32, 64):
        tail = tail + pltpu.roll(tail, shift, 1)
    tail = jnp.where((row + lane // 16) % 8 == 0, tail, 0.0)
    tail = jnp.sum(tail.reshape(2, 8, 128), axis=1)
    put(out, t, jnp.concatenate([value[:, 0:128], tail], axis=0))


def unpack(ref, t):
    packed = get(ref, t)
    tail = jnp.broadcast_to(packed[R:ROWS, None, :], (2, 8, 128)).reshape(R, 128)
    tail = pltpu.roll(tail, 0, 1, stride=16, stride_axis=0)
    return jnp.concatenate([packed[0:R], tail[:, 0:16]], axis=1)


def pieces(x):
    high = x.astype(BF)
    rest = x - high.astype(F32)
    mid = rest.astype(BF)
    low = (rest - mid.astype(F32)).astype(BF)
    return jnp.concatenate([high, mid, low], axis=0)


def gather3(x):
    return x[0:R] + x[R : 2 * R] + x[2 * R : 3 * R]


def rows_times(a, b):
    return lax.dot_general(a, b, (((1,), (1,)), ((), ())), preferred_element_type=F32)


def main_kernel(
    res_inner_h, res_face_h, inner_inv_h, coupling_h, face_inv_h, basis_h, coarse_inv_h,
    map_row_own, index_row, sharers, elem,
    rows_h, terms_h,
    res_inner, inner_inv, inner_w, res_face, face_rows, stage, coupling, face_inv, basis_stage, basis,
    coarse_inv, coarse_high, coarse_low, pick, own_pick, maps,
    sent, received, wide, wide2, back, gathered, gathered2, restricted, local,
    part, part_in, share, share_in, chosen, chosen_in, map_block, weight, contrast,
    rows_out, terms_out, out_sems, entered, piece_sems, batch_sems, load_sems, send_sems, recv_sems, own_sems,
):
    sub = lax.axis_index("sub")
    grp = lax.axis_index("grp")
    me = sub * GRP + grp
    barrier = pltpu.get_barrier_semaphore()

    def load(src, dst, k):
        return pltpu.make_async_copy(src, dst, load_sems.at[k])

    load(res_inner_h, res_inner, 0).start()

    def piece(src, dst, q, k):
        rows = pl.ds(pl.multiple_of(q * 16, 16), 16)
        return pltpu.make_async_copy(src.at[rows], dst.at[rows], piece_sems.at[k + q])

    def inverse_piece(q):
        return piece(inner_inv_h, inner_inv, q, 0)

    def coupling_piece(q):
        return piece(coupling_h, stage, q, 4)

    for q in range(4):
        inverse_piece(q).start()
    load(res_face_h, res_face, 3).start()
    for q in range(9):
        coupling_piece(q).start()

    def signal(semaphore, device):
        pl.semaphore_signal(semaphore, inc=1, device_id=device, device_id_type=MESH)

    def each(first, last, f, unroll=1):
        def one(i, c):
            f(i)
            return c

        lax.fori_loop(first, last, one, 0, unroll=unroll)

    each(1, GRP, lambda i: signal(barrier, (sub, lax.rem(grp + i, GRP))))
    each(1, SUB, lambda i: signal(barrier, (lax.rem(sub + i, SUB), grp)))

    def tall(row):
        return jnp.broadcast_to(row, (N, N)).T

    counts = sharers[...]
    weight[...] = tall(jnp.where(counts > 0, 1.0 / jnp.maximum(counts, 1).astype(F32), 0.0))
    map_own = jnp.concatenate([map_row_own[...], jnp.zeros((1, 128 - NC), jnp.int32)], axis=1)
    map_block[...] = jnp.broadcast_to(map_own, (8, 128))
    index = index_row[...].astype(F32)
    contrast[...] = jnp.where((index == tall(index)) & (index < 32.0), 1.0, 0.0).astype(BF)

    def inner(e):
        inner_w[e] = rows_times(res_inner[e], inner_inv[e]).astype(BF)

    load(res_inner_h, res_inner, 0).wait()

    def inners(q):
        inverse_piece(q).wait()
        for e in range(16):
            inner(16 * q + e)

    each(0, 4, inners)
    pl.semaphore_wait(barrier, GRP + SUB - 2)
    each(1, SUB, lambda i: signal(entered, (lax.rem(sub + i, SUB), grp)))

    def turn(src, dst, q):
        part_rows = src[pl.ds(pl.multiple_of(q * 16, 16), 16)]
        part_rows = jnp.swapaxes(jnp.swapaxes(part_rows, 1, 2), 0, 1)
        dst[:, pl.ds(pl.multiple_of(q * 16, 16), 16), :] = part_rows

    def turns(src, dst, first, last):
        def one(q, c):
            turn(src, dst, q)
            return c

        lax.fori_loop(first, last, one, 0)

    load(res_face_h, res_face, 3).wait()
    turns(res_face, face_rows, 0, 1)

    def coupling_turn(q):
        coupling_piece(q).wait()
        turn(stage, coupling, q)

    each(0, 9, coupling_turn)
    load(face_inv_h, stage, 6).start()
    load(basis_h, basis_stage, 4).start()
    load(coarse_inv_h, coarse_inv, 5).start()

    pl.semaphore_wait(entered, SUB - 1)

    def map_copy(i):
        return remote(map_block, maps.at[grp], (sub, lax.rem(grp + i, GRP)), send_sems.at[0], recv_sems.at[0])

    own_map = pltpu.make_async_copy(map_block, maps.at[grp], own_sems.at[0])
    own_map.start()
    each(1, GRP, lambda i: map_copy(i).start())

    def quad(i):
        return lax.rem(me // 4 + i, N // 4) * 4

    def exchange(source, target, k, fill, arrived):
        def give(t, q):
            remote(source.at[t], target.at[me], place(t), send_sems.at[k], arrived(q)).start()

        def batch(q):
            for i in range(4):
                fill(quad(q * 4 + i))

        batch(0)
        own = pltpu.make_async_copy(source.at[me], target.at[me], own_sems.at[k])
        own.start()
        each(1, 4, lambda j: give(quad(0) + lax.rem(me + j, 4), 0))
        each(4, 16, lambda j: give(quad(j // 4) + lax.rem(me + j, 4), 0))

        def more(q):
            batch(q)
            each(16 * q, 16 * q + 16, lambda j: give(quad(j // 4) + lax.rem(me + j, 4), q))

        each(1, N // 16, more)
        return own

    def all_at_once(k):
        return lambda q: recv_sems.at[k]

    def in_batches(c):
        return lambda q: batch_sems.at[c * 8 + q]

    def sent_all(source, k):
        rest = source.at[pl.ds(0, N - 1)]
        remote(rest, rest, (sub, grp), send_sems.at[k], recv_sems.at[k]).wait_send()

    def arrive(source, target, k, own):
        own.wait()
        rest = target.at[pl.ds(0, N - 1)]
        remote(rest, rest, (sub, grp), send_sems.at[k], recv_sems.at[k]).wait_recv()
        sent_all(source, k)

    def arrive_in_batches(source, target, k, own, arrived, use, carry):
        def wait(q, count):
            some = target.at[pl.ds(0, count)]
            remote(some, some, (sub, grp), send_sems.at[k], arrived(q)).wait_recv()

        def use_batch(q, carry):
            return use([quad(N // 4 - 4 * q - i) for i in range(4)], carry)

        def next_batch(q, carry):
            wait(q, 16)
            return use_batch(q, carry)

        own.wait()
        wait(0, 15)
        carry = lax.fori_loop(1, N // 16, next_batch, use_batch(0, carry))
        sent_all(source, k)
        return carry

    def scaled(t, value):
        scale = jnp.broadcast_to(weight[pl.ds(t, 1), :], (R, 128))
        return jnp.concatenate([scale, scale[:, 0:16]], axis=1) * value

    def condense(base):
        for t in [base + k for k in range(4)]:
            product = rows_times(inner_w[elem[0, t]], coupling[t])
            pack(sent, t, scaled(t, face_rows[t].astype(F32) - product))

    own = exchange(sent, received.at[0], 1, condense, all_at_once(1))
    load(face_inv_h, stage, 6).wait()
    turns(stage, face_inv, 0, 8)
    arrive(sent, received.at[0], 1, own)

    same = contrast[...]

    def owner_sum(source):
        def widen(s):
            wide[pl.ds(pl.multiple_of(s * PITCH, 8), ROWS)] = get(source, s)

        each(0, N, widen, 8)
        for k in range(ROWS):
            rows = wide[pl.ds(k, N, stride=PITCH), :].astype(BF)
            wide2[pl.ds(k, N, stride=PITCH), :] = jnp.dot(same, rows, preferred_element_type=F32)

    def narrow(target):
        def one(base):
            for t in [base + k for k in range(4)]:
                put(target, t, wide2[pl.ds(pl.multiple_of(t * PITCH, 8), ROWS)])

        return one

    owner_sum(received.at[0])
    own = exchange(back, gathered, 2, narrow(back), in_batches(0))

    turns(stage, face_inv, 8, 9)
    load(basis_h, basis_stage, 4).wait()
    turns(basis_stage, basis, 0, 4)
    load(coarse_inv_h, coarse_inv, 5).wait()

    def split(q):
        rows = pl.ds(pl.multiple_of(q * 16, 16), 16)
        high = coarse_inv[rows, :].astype(BF)
        coarse_high[rows, :] = high
        coarse_low[rows, :] = (coarse_inv[rows, :] - high.astype(F32)).astype(BF)

    each(0, SHARE // 16, split)
    own_map.wait()
    seven = pl.ds(0, GRP - 1)
    remote(maps.at[seven], maps.at[seven], (sub, grp), send_sems.at[0], recv_sems.at[0]).wait()
    map_row = jnp.concatenate([maps[g, 0:1, 0:NC] for g in range(GRP)], axis=1)

    def mark(q):
        at = lax.broadcasted_iota(jnp.int32, (128, GRP * NC), 0) + q * 128
        pick[pl.ds(pl.multiple_of(q * 128, 128), 128), :] = jnp.where(map_row == at, 1.0, 0.0).astype(BF)

    each(0, NCG // 128, mark)
    map_tall = tall(map_own.astype(F32))[0:NC]
    for q in range(NCG // 128):
        at = (lax.broadcasted_iota(jnp.int32, (NC, 128), 1) + q * 128).astype(F32)
        own_pick[:, q * 128 : (q + 1) * 128] = jnp.where(map_tall == at, 1.0, 0.0).astype(BF)

    def basis4(q):
        return basis[pl.ds(pl.multiple_of(q * 4, 4), 4)].reshape(4 * NC, B)

    def project(bases, total):
        for base in bases:
            rows = []
            for t in [base + k for k in range(4)]:
                rows.append(scaled(t, unpack(gathered, t)).astype(BF))
                restricted[t] = rows[-1]
            total = total + rows_times(jnp.concatenate(rows, axis=0), basis4(base // 4))
        return total

    crossed = arrive_in_batches(
        back, gathered, 2, own, in_batches(0), project, jnp.zeros((4 * R, 4 * NC), F32)
    )
    local_coarse = sum(crossed[k * R : (k + 1) * R, k * NC : (k + 1) * NC] for k in range(4))

    partial = gather3(jnp.dot(pieces(local_coarse), own_pick[...], preferred_element_type=F32))
    for g in range(GRP):
        part[g] = partial[:, g * SHARE : (g + 1) * SHARE]

    own = pltpu.make_async_copy(part.at[grp], part_in.at[grp], own_sems.at[3])
    own.start()

    def ring_send(source, target, k):
        def one(i):
            t = lax.rem(grp + i, GRP)
            remote(source.at[t], target.at[grp], (sub, t), send_sems.at[k], recv_sems.at[k]).start()

        each(1, GRP, one)

    def ring_wait(source, target, k):
        remote(source.at[seven], target.at[seven], (sub, grp), send_sems.at[k], recv_sems.at[k]).wait()

    def solve_local(t):
        local[t] = rows_times(restricted[t], face_inv[t])

    ring_send(part, part_in, 3)
    each(0, 64, solve_local, 8)
    own.wait()
    ring_wait(part, part_in, 3)
    share[...] = jnp.sum(part_in[...], axis=0)
    own = pltpu.make_async_copy(share, share_in.at[sub], own_sems.at[4])
    own.start()

    def share_copy(i):
        t = lax.rem(sub + i, SUB)
        remote(share, share_in.at[sub], (t, grp), send_sems.at[4], recv_sems.at[4]).start()

    each(1, SUB, share_copy)
    each(64, N, solve_local, 8)
    own.wait()
    fifteen = pl.ds(0, SUB - 1)
    remote(share_in.at[fifteen], share_in.at[fifteen], (sub, grp), send_sems.at[4], recv_sems.at[4]).wait()
    total = pieces(jnp.sum(share_in[...], axis=0))
    term = gather3(
        jnp.dot(total, coarse_high[...], preferred_element_type=F32)
        + jnp.dot(total, coarse_low[...], preferred_element_type=F32)
    )
    picked = gather3(jnp.dot(pieces(term), pick[...], preferred_element_type=F32))
    for g in range(GRP):
        chosen[g, :, 0:NC] = picked[:, g * NC : (g + 1) * NC]
        chosen[g, :, NC:128] = jnp.zeros((R, 128 - NC), F32)
    own = pltpu.make_async_copy(chosen.at[grp], chosen_in.at[grp], own_sems.at[5])
    own.start()
    ring_send(chosen, chosen_in, 5)
    own.wait()
    ring_wait(chosen, chosen_in, 5)
    mine = jnp.sum(chosen_in[...], axis=0)[:, 0:NC]
    row = lax.broadcasted_iota(jnp.int32, (4 * R, 4 * NC), 0) // R
    lane = lax.broadcasted_iota(jnp.int32, (4 * R, 4 * NC), 1) // NC
    mine4 = jnp.concatenate([jnp.concatenate([mine] * 4, axis=1)] * 4, axis=0)
    mine4 = jnp.where(row == lane, mine4, 0.0).astype(BF)

    def correct(base):
        coarse = jnp.dot(mine4, basis4(base // 4), preferred_element_type=F32)
        for k in range(4):
            pack(sent, base + k, scaled(base + k, local[base + k] + coarse[k * R : (k + 1) * R]))

    own = exchange(sent, received.at[1], 6, correct, all_at_once(6))
    arrive(sent, received.at[1], 6, own)
    owner_sum(received.at[1])
    own = exchange(back, gathered2, 7, narrow(back), in_batches(1))

    def extend(bases, carry):
        for base in bases:
            for t in [base + k for k in range(4)]:
                rows = unpack(gathered2, t).astype(BF)
                rows_out[t] = rows
                terms_out[t] = jnp.dot(rows, coupling[t], preferred_element_type=F32)
        for base in bases:
            four = pl.ds(base, 4)
            pltpu.make_async_copy(rows_out.at[four], rows_h.at[four], out_sems.at[0]).start()
            pltpu.make_async_copy(terms_out.at[four], terms_h.at[four], out_sems.at[1]).start()
        return carry

    arrive_in_batches(back, gathered2, 7, own, in_batches(1), extend, 0)
    pltpu.make_async_copy(rows_out, rows_h, out_sems.at[0]).wait()
    pltpu.make_async_copy(terms_out, terms_h, out_sems.at[1]).wait()


def extend_kernel(
    elem, rows_h, terms_h, res_inner_h, inner_inv_h, inner_out, face_out,
    rows, terms, res_inner, total, inner_inv, sems,
):
    pairs = ((res_inner_h, res_inner), (terms_h, terms), (rows_h, rows), (inner_inv_h, inner_inv))
    loads = [pltpu.make_async_copy(src, dst, sems.at[k]) for k, (src, dst) in enumerate(pairs)]
    for one in loads:
        one.start()
    loads[0].wait()
    total[...] = res_inner[...].astype(F32)
    loads[1].wait()

    def add(t, c):
        e = elem[0, t]
        total[e] = total[e] - terms[t]
        return c

    lax.fori_loop(0, N, add, 0, unroll=8)
    loads[2].wait()
    face_out[...] = jnp.swapaxes(jnp.swapaxes(rows[...], 0, 1), 1, 2)
    loads[3].wait()

    def inner(e, c):
        inner_out[e] = rows_times(total[e].astype(BF), inner_inv[e]).astype(BF)
        return c

    lax.fori_loop(0, E, inner, 0, unroll=16)


def body(
    res_inner, res_face, inner_inv, face_coupling, face_elem, face_inv, coarse_basis, coarse_map, coarse_inv,
    recv_index, sharers,
):
    vm = pl.BlockSpec(memory_space=pltpu.VMEM)
    hbm = pl.BlockSpec(memory_space=pl.ANY)
    sm = pl.BlockSpec(memory_space=pltpu.SMEM)
    slots_last = (1, 2, 0)
    packed = (N, ROWS // 2, 2, 128)
    rows, terms = pl.pallas_call(
        main_kernel,
        out_shape=(jax.ShapeDtypeStruct((N, R, B), BF), jax.ShapeDtypeStruct((N, R, B), F32)),
        in_specs=[hbm] * 7 + [vm] * 3 + [sm],
        out_specs=(hbm, hbm),
        scratch_shapes=[
            pltpu.VMEM((E, R, B), BF),
            pltpu.VMEM((E, B, B), BF),
            pltpu.VMEM((E, R, B), BF),
            pltpu.VMEM((R, B, N), BF),
            pltpu.VMEM((N, R, B), BF),
            pltpu.VMEM((B, B, N), BF),
            pltpu.VMEM((N, B, B), BF),
            pltpu.VMEM((N, B, B), BF),
            pltpu.VMEM((NC, B, N), BF),
            pltpu.VMEM((N, NC, B), BF),
            pltpu.VMEM((SHARE, NCG), F32),
            pltpu.VMEM((SHARE, NCG), BF),
            pltpu.VMEM((SHARE, NCG), BF),
            pltpu.VMEM((NCG, GRP * NC), BF),
            pltpu.VMEM((NC, NCG), BF),
            pltpu.VMEM((GRP, 8, 128), jnp.int32),
            pltpu.VMEM(packed, BF),
            pltpu.VMEM((2, *packed), BF),
            pltpu.VMEM((N * PITCH, 128), F32),
            pltpu.VMEM((N * PITCH, 128), F32),
            pltpu.VMEM(packed, BF),
            pltpu.VMEM(packed, BF),
            pltpu.VMEM(packed, BF),
            pltpu.VMEM((N, R, B), BF),
            pltpu.VMEM((N, R, B), F32),
            pltpu.VMEM((GRP, R, SHARE), F32),
            pltpu.VMEM((GRP, R, SHARE), F32),
            pltpu.VMEM((R, SHARE), F32),
            pltpu.VMEM((SUB, R, SHARE), F32),
            pltpu.VMEM((GRP, R, 128), F32),
            pltpu.VMEM((GRP, R, 128), F32),
            pltpu.VMEM((8, 128), jnp.int32),
            pltpu.VMEM((N, N), F32),
            pltpu.VMEM((N, N), BF),
            pltpu.VMEM((N, R, B), BF),
            pltpu.VMEM((N, R, B), F32),
            pltpu.SemaphoreType.DMA((2,)),
            pltpu.SemaphoreType.REGULAR,
            pltpu.SemaphoreType.DMA((16,)),
            pltpu.SemaphoreType.DMA((16,)),
            pltpu.SemaphoreType.DMA((8,)),
            pltpu.SemaphoreType.DMA((8,)),
            pltpu.SemaphoreType.DMA((8,)),
            pltpu.SemaphoreType.DMA((8,)),
        ],
        name="assemble_all",
        compiler_params=pltpu.CompilerParams(
            collective_id=0, has_side_effects=True, vmem_limit_bytes=61 << 20
        ),
    )(
        res_inner,
        jnp.transpose(res_face, slots_last),
        inner_inv,
        jnp.transpose(face_coupling, slots_last),
        jnp.transpose(face_inv, slots_last),
        jnp.transpose(coarse_basis, slots_last),
        coarse_inv,
        coarse_map,
        recv_index,
        sharers,
        face_elem,
    )
    inner_out, face_out = pl.pallas_call(
        extend_kernel,
        out_shape=(jax.ShapeDtypeStruct((E, R, B), BF), jax.ShapeDtypeStruct((R, B, N), BF)),
        in_specs=[sm, hbm, hbm, hbm, hbm],
        out_specs=(vm, vm),
        scratch_shapes=[
            pltpu.VMEM((N, R, B), BF),
            pltpu.VMEM((N, R, B), F32),
            pltpu.VMEM((E, R, B), BF),
            pltpu.VMEM((E, R, B), F32),
            pltpu.VMEM((E, B, B), BF),
            pltpu.SemaphoreType.DMA((4,)),
        ],
        name="extend",
        compiler_params=pltpu.CompilerParams(vmem_limit_bytes=61 << 20),
    )(face_elem, rows, terms, res_inner, inner_inv)
    return inner_out, jnp.transpose(face_out, (2, 0, 1))


def solution(mesh):
    split = P(("sub", "grp"), None, None)
    table = P(("sub", "grp"), None)
    return jax.shard_map(
        body,
        mesh=mesh,
        in_specs=(
            split, split, split, split, table, split, split, table, P("grp", None), table, table,
        ),
        out_specs=(split, split),
        check_vma=False,
    )
```

```python
import jax
import jax.numpy as jnp
from jax import lax
from jax.experimental import pallas as pl
from jax.experimental.pallas import tpu as pltpu
from jax.sharding import PartitionSpec as P

MESH = pl.DeviceIdType.MESH
N = 128
E = 64
R = 16
B = 144
NC = 64
NCG = 2048
GRP = 8
SUB = 16
SHARE = NCG // GRP
ROWS = 18
PITCH = 24
BF = jnp.bfloat16
F32 = jnp.float32


def place(t):
    return (t // GRP, t % GRP)


def remote(src, dst, device, s, r):
    return pltpu.make_async_remote_copy(
        src_ref=src, dst_ref=dst, send_sem=s, recv_sem=r, device_id=device, device_id_type=MESH
    )


def put(out, t, rows):
    out[t] = rows.reshape(ROWS // 2, 2, 128).astype(BF)


def get(ref, t):
    return ref[t].reshape(ROWS, 128).astype(F32)


def pack(out, t, value):
    row = lax.broadcasted_iota(jnp.int32, (R, 128), 0)
    lane = lax.broadcasted_iota(jnp.int32, (R, 128), 1)
    tail = jnp.concatenate([value[:, 128:B], jnp.zeros((R, 112), F32)], axis=1)
    for shift in (16, 32, 64):
        tail = tail + pltpu.roll(tail, shift, 1)
    tail = jnp.where((row + lane // 16) % 8 == 0, tail, 0.0)
    tail = jnp.sum(tail.reshape(2, 8, 128), axis=1)
    put(out, t, jnp.concatenate([value[:, 0:128], tail], axis=0))


def unpack(ref, t):
    packed = get(ref, t)
    tail = jnp.broadcast_to(packed[R:ROWS, None, :], (2, 8, 128)).reshape(R, 128)
    tail = pltpu.roll(tail, 0, 1, stride=16, stride_axis=0)
    return jnp.concatenate([packed[0:R], tail[:, 0:16]], axis=1)


def pieces(x):
    high = x.astype(BF)
    rest = x - high.astype(F32)
    mid = rest.astype(BF)
    low = (rest - mid.astype(F32)).astype(BF)
    return jnp.concatenate([high, mid, low], axis=0)


def gather3(x):
    return x[0:R] + x[R : 2 * R] + x[2 * R : 3 * R]


def rows_times(a, b):
    return lax.dot_general(a, b, (((1,), (1,)), ((), ())), preferred_element_type=F32)


def main_kernel(
    res_inner_h, res_face_h, inner_inv_h, coupling_h, face_inv_h, basis_h, coarse_inv_h,
    map_row_own, index_row, sharers, elem,
    rows_h, terms_h,
    res_inner, inner_inv, inner_w, res_face, face_rows, stage, coupling, face_inv, basis_stage, basis,
    coarse_inv, coarse_high, coarse_low, pick, own_pick, maps,
    sent, received, wide, wide2, back, gathered, gathered2, restricted, local,
    part, part_in, share, share_in, chosen, chosen_in, map_block, weight, contrast,
    rows_out, terms_out, out_sems, entered, piece_sems, batch_sems, load_sems, send_sems, recv_sems, own_sems,
):
    sub = lax.axis_index("sub")
    grp = lax.axis_index("grp")
    me = sub * GRP + grp
    barrier = pltpu.get_barrier_semaphore()

    def load(src, dst, k):
        return pltpu.make_async_copy(src, dst, load_sems.at[k])

    load(res_inner_h, res_inner, 0).start()

    def piece(src, dst, q, k):
        rows = pl.ds(pl.multiple_of(q * 16, 16), 16)
        return pltpu.make_async_copy(src.at[rows], dst.at[rows], piece_sems.at[k + q])

    def inverse_piece(q):
        return piece(inner_inv_h, inner_inv, q, 0)

    def coupling_piece(q):
        return piece(coupling_h, stage, q, 4)

    for q in range(9):
        coupling_piece(q).start()
    for q in range(4):
        inverse_piece(q).start()
    load(res_face_h, res_face, 3).start()

    def signal(semaphore, device):
        pl.semaphore_signal(semaphore, inc=1, device_id=device, device_id_type=MESH)

    def each(first, last, f, unroll=1):
        def one(i, c):
            f(i)
            return c

        lax.fori_loop(first, last, one, 0, unroll=unroll)

    each(1, GRP, lambda i: signal(barrier, (sub, lax.rem(grp + i, GRP))))
    each(1, SUB, lambda i: signal(barrier, (lax.rem(sub + i, SUB), grp)))

    def tall(row):
        return jnp.broadcast_to(row, (N, N)).T

    counts = sharers[...]
    weight[...] = tall(jnp.where(counts > 0, 1.0 / jnp.maximum(counts, 1).astype(F32), 0.0))
    map_own = jnp.concatenate([map_row_own[...], jnp.zeros((1, 128 - NC), jnp.int32)], axis=1)
    map_block[...] = jnp.broadcast_to(map_own, (8, 128))
    index = index_row[...].astype(F32)
    contrast[...] = jnp.where((index == tall(index)) & (index < 32.0), 1.0, 0.0).astype(BF)

    def turn(src, dst, q):
        part_rows = src[pl.ds(pl.multiple_of(q * 16, 16), 16)]
        part_rows = jnp.swapaxes(jnp.swapaxes(part_rows, 1, 2), 0, 1)
        dst[:, pl.ds(pl.multiple_of(q * 16, 16), 16), :] = part_rows

    def turns(src, dst, first, last):
        def one(q, c):
            turn(src, dst, q)
            return c

        lax.fori_loop(first, last, one, 0)

    def coupling_turn(q):
        coupling_piece(q).wait()
        turn(stage, coupling, q)

    each(0, 9, coupling_turn)
    load(face_inv_h, stage, 6).start()
    pl.semaphore_wait(barrier, GRP + SUB - 2)
    each(1, SUB, lambda i: signal(entered, (lax.rem(sub + i, SUB), grp)))

    def inner(e):
        inner_w[e] = rows_times(res_inner[e], inner_inv[e]).astype(BF)

    load(res_inner_h, res_inner, 0).wait()

    def inners(q):
        inverse_piece(q).wait()
        for e in range(16):
            inner(16 * q + e)

    each(0, 4, inners)
    load(basis_h, basis_stage, 4).start()
    load(coarse_inv_h, coarse_inv, 5).start()
    load(res_face_h, res_face, 3).wait()
    turns(res_face, face_rows, 0, 1)
    pl.semaphore_wait(entered, SUB - 1)

    def map_copy(i):
        return remote(map_block, maps.at[grp], (sub, lax.rem(grp + i, GRP)), send_sems.at[0], recv_sems.at[0])

    own_map = pltpu.make_async_copy(map_block, maps.at[grp], own_sems.at[0])
    own_map.start()
    each(1, GRP, lambda i: map_copy(i).start())

    def quad(i):
        return lax.rem(me // 4 + i, N // 4) * 4

    def exchange(source, target, k, fill, arrived, size):
        def give(t, j):
            remote(source.at[t], target.at[me], place(t), send_sems.at[k], arrived(j // 16)).start()

        def batch(q):
            for i in range(size // 4):
                fill(quad(q * (size // 4) + i))

        def pass_on(j):
            give(quad(j // 4) + lax.rem(me + j, 4), j)

        batch(0)
        own = pltpu.make_async_copy(source.at[me], target.at[me], own_sems.at[k])
        own.start()
        each(1, size, pass_on)

        def more(q):
            batch(q)
            each(size * q, size * q + size, pass_on)

        each(1, N // size, more)
        return own

    def all_at_once(k):
        return lambda q: recv_sems.at[k]

    def in_batches(c):
        return lambda q: batch_sems.at[c * 8 + q]

    def sent_all(source, k):
        rest = source.at[pl.ds(0, N - 1)]
        remote(rest, rest, (sub, grp), send_sems.at[k], recv_sems.at[k]).wait_send()

    def arrive(source, target, k, own):
        own.wait()
        rest = target.at[pl.ds(0, N - 1)]
        remote(rest, rest, (sub, grp), send_sems.at[k], recv_sems.at[k]).wait_recv()
        sent_all(source, k)

    def arrive_in_batches(source, target, k, own, arrived, use, carry):
        def wait(q, count):
            some = target.at[pl.ds(0, count)]
            remote(some, some, (sub, grp), send_sems.at[k], arrived(q)).wait_recv()

        def use_batch(q, carry):
            return use([quad(N // 4 - 4 * q - i) for i in range(4)], carry)

        def next_batch(q, carry):
            wait(q, 16)
            return use_batch(q, carry)

        own.wait()
        wait(0, 15)
        carry = lax.fori_loop(1, N // 16, next_batch, use_batch(0, carry))
        sent_all(source, k)
        return carry

    def scaled(t, value):
        scale = jnp.broadcast_to(weight[pl.ds(t, 1), :], (R, 128))
        return jnp.concatenate([scale, scale[:, 0:16]], axis=1) * value

    def condense(base):
        for t in [base + k for k in range(4)]:
            product = rows_times(inner_w[elem[0, t]], coupling[t])
            pack(sent, t, scaled(t, face_rows[t].astype(F32) - product))

    own = exchange(sent, received.at[0], 1, condense, all_at_once(1), 32)
    load(face_inv_h, stage, 6).wait()
    turns(stage, face_inv, 0, 8)
    arrive(sent, received.at[0], 1, own)

    same = contrast[...]

    def owner_sum(source):
        def widen(s):
            wide[pl.ds(pl.multiple_of(s * PITCH, 8), ROWS)] = get(source, s)

        each(0, N, widen, 8)
        for k in range(ROWS):
            rows = wide[pl.ds(k, N, stride=PITCH), :].astype(BF)
            wide2[pl.ds(k, N, stride=PITCH), :] = jnp.dot(same, rows, preferred_element_type=F32)

    def narrow(target):
        def one(base):
            for t in [base + k for k in range(4)]:
                put(target, t, wide2[pl.ds(pl.multiple_of(t * PITCH, 8), ROWS)])

        return one

    owner_sum(received.at[0])
    own = exchange(back, gathered, 2, narrow(back), in_batches(0), 16)

    turns(stage, face_inv, 8, 9)
    load(basis_h, basis_stage, 4).wait()
    turns(basis_stage, basis, 0, 4)
    load(coarse_inv_h, coarse_inv, 5).wait()

    def split(q):
        rows = pl.ds(pl.multiple_of(q * 16, 16), 16)
        high = coarse_inv[rows, :].astype(BF)
        coarse_high[rows, :] = high
        coarse_low[rows, :] = (coarse_inv[rows, :] - high.astype(F32)).astype(BF)

    each(0, SHARE // 16, split)
    own_map.wait()
    seven = pl.ds(0, GRP - 1)
    remote(maps.at[seven], maps.at[seven], (sub, grp), send_sems.at[0], recv_sems.at[0]).wait()
    map_row = jnp.concatenate([maps[g, 0:1, 0:NC] for g in range(GRP)], axis=1)

    def mark(q):
        at = lax.broadcasted_iota(jnp.int32, (128, GRP * NC), 0) + q * 128
        pick[pl.ds(pl.multiple_of(q * 128, 128), 128), :] = jnp.where(map_row == at, 1.0, 0.0).astype(BF)

    each(0, NCG // 128, mark)
    map_tall = tall(map_own.astype(F32))[0:NC]
    for q in range(NCG // 128):
        at = (lax.broadcasted_iota(jnp.int32, (NC, 128), 1) + q * 128).astype(F32)
        own_pick[:, q * 128 : (q + 1) * 128] = jnp.where(map_tall == at, 1.0, 0.0).astype(BF)

    def basis4(q):
        return basis[pl.ds(pl.multiple_of(q * 4, 4), 4)].reshape(4 * NC, B)

    def project(bases, total):
        for base in bases:
            rows = []
            for t in [base + k for k in range(4)]:
                rows.append(scaled(t, unpack(gathered, t)).astype(BF))
                restricted[t] = rows[-1]
            total = total + rows_times(jnp.concatenate(rows, axis=0), basis4(base // 4))
        return total

    crossed = arrive_in_batches(
        back, gathered, 2, own, in_batches(0), project, jnp.zeros((4 * R, 4 * NC), F32)
    )
    local_coarse = sum(crossed[k * R : (k + 1) * R, k * NC : (k + 1) * NC] for k in range(4))

    partial = gather3(jnp.dot(pieces(local_coarse), own_pick[...], preferred_element_type=F32))
    for g in range(GRP):
        part[g] = partial[:, g * SHARE : (g + 1) * SHARE]

    own = pltpu.make_async_copy(part.at[grp], part_in.at[grp], own_sems.at[3])
    own.start()

    def ring_send(source, target, k):
        def one(i):
            t = lax.rem(grp + i, GRP)
            remote(source.at[t], target.at[grp], (sub, t), send_sems.at[k], recv_sems.at[k]).start()

        each(1, GRP, one)

    def ring_wait(source, target, k):
        remote(source.at[seven], target.at[seven], (sub, grp), send_sems.at[k], recv_sems.at[k]).wait()

    def solve_local(t):
        local[t] = rows_times(restricted[t], face_inv[t])

    ring_send(part, part_in, 3)
    each(0, 64, solve_local, 32)
    own.wait()
    ring_wait(part, part_in, 3)
    share[...] = jnp.sum(part_in[...], axis=0)
    own = pltpu.make_async_copy(share, share_in.at[sub], own_sems.at[4])
    own.start()

    def share_copy(i):
        t = lax.rem(sub + i, SUB)
        remote(share, share_in.at[sub], (t, grp), send_sems.at[4], recv_sems.at[4]).start()

    each(1, SUB, share_copy)
    each(64, N, solve_local, 32)
    own.wait()
    fifteen = pl.ds(0, SUB - 1)
    remote(share_in.at[fifteen], share_in.at[fifteen], (sub, grp), send_sems.at[4], recv_sems.at[4]).wait()
    total = pieces(jnp.sum(share_in[...], axis=0))
    term = gather3(
        jnp.dot(total, coarse_high[...], preferred_element_type=F32)
        + jnp.dot(total, coarse_low[...], preferred_element_type=F32)
    )
    picked = gather3(jnp.dot(pieces(term), pick[...], preferred_element_type=F32))
    for g in range(GRP):
        chosen[g, :, 0:NC] = picked[:, g * NC : (g + 1) * NC]
        chosen[g, :, NC:128] = jnp.zeros((R, 128 - NC), F32)
    own = pltpu.make_async_copy(chosen.at[grp], chosen_in.at[grp], own_sems.at[5])
    own.start()
    ring_send(chosen, chosen_in, 5)
    own.wait()
    ring_wait(chosen, chosen_in, 5)
    mine = jnp.sum(chosen_in[...], axis=0)[:, 0:NC]
    row = lax.broadcasted_iota(jnp.int32, (4 * R, 4 * NC), 0) // R
    lane = lax.broadcasted_iota(jnp.int32, (4 * R, 4 * NC), 1) // NC
    mine4 = jnp.concatenate([jnp.concatenate([mine] * 4, axis=1)] * 4, axis=0)
    mine4 = jnp.where(row == lane, mine4, 0.0).astype(BF)

    def correct(base):
        coarse = jnp.dot(mine4, basis4(base // 4), preferred_element_type=F32)
        for k in range(4):
            pack(sent, base + k, scaled(base + k, local[base + k] + coarse[k * R : (k + 1) * R]))

    own = exchange(sent, received.at[1], 6, correct, all_at_once(6), 32)
    arrive(sent, received.at[1], 6, own)
    owner_sum(received.at[1])
    own = exchange(back, gathered2, 7, narrow(back), in_batches(1), 16)

    def extend(bases, carry):
        for base in bases:
            for t in [base + k for k in range(4)]:
                rows = unpack(gathered2, t).astype(BF)
                rows_out[t] = rows
                terms_out[t] = jnp.dot(rows, coupling[t], preferred_element_type=F32)
        for base in bases:
            four = pl.ds(base, 4)
            pltpu.make_async_copy(rows_out.at[four], rows_h.at[four], out_sems.at[0]).start()
            pltpu.make_async_copy(terms_out.at[four], terms_h.at[four], out_sems.at[1]).start()
        return carry

    arrive_in_batches(back, gathered2, 7, own, in_batches(1), extend, 0)
    pltpu.make_async_copy(rows_out, rows_h, out_sems.at[0]).wait()
    pltpu.make_async_copy(terms_out, terms_h, out_sems.at[1]).wait()


def extend_kernel(
    elem, rows_h, terms_h, res_inner_h, inner_inv_h, inner_out, face_out,
    rows, terms, res_inner, total, inner_inv, sems,
):
    pairs = ((res_inner_h, res_inner), (terms_h, terms), (rows_h, rows), (inner_inv_h, inner_inv))
    loads = [pltpu.make_async_copy(src, dst, sems.at[k]) for k, (src, dst) in enumerate(pairs)]
    for one in loads:
        one.start()
    loads[0].wait()
    total[...] = res_inner[...].astype(F32)
    loads[1].wait()

    def add(t, c):
        e = elem[0, t]
        total[e] = total[e] - terms[t]
        return c

    lax.fori_loop(0, N, add, 0, unroll=8)
    loads[2].wait()
    face_out[...] = jnp.swapaxes(jnp.swapaxes(rows[...], 0, 1), 1, 2)
    loads[3].wait()

    def inner(e, c):
        inner_out[e] = rows_times(total[e].astype(BF), inner_inv[e]).astype(BF)
        return c

    lax.fori_loop(0, E, inner, 0, unroll=32)


def body(
    res_inner, res_face, inner_inv, face_coupling, face_elem, face_inv, coarse_basis, coarse_map, coarse_inv,
    recv_index, sharers,
):
    vm = pl.BlockSpec(memory_space=pltpu.VMEM)
    hbm = pl.BlockSpec(memory_space=pl.ANY)
    sm = pl.BlockSpec(memory_space=pltpu.SMEM)
    slots_last = (1, 2, 0)
    packed = (N, ROWS // 2, 2, 128)
    rows, terms = pl.pallas_call(
        main_kernel,
        out_shape=(jax.ShapeDtypeStruct((N, R, B), BF), jax.ShapeDtypeStruct((N, R, B), F32)),
        in_specs=[hbm] * 7 + [vm] * 3 + [sm],
        out_specs=(hbm, hbm),
        scratch_shapes=[
            pltpu.VMEM((E, R, B), BF),
            pltpu.VMEM((E, B, B), BF),
            pltpu.VMEM((E, R, B), BF),
            pltpu.VMEM((R, B, N), BF),
            pltpu.VMEM((N, R, B), BF),
            pltpu.VMEM((B, B, N), BF),
            pltpu.VMEM((N, B, B), BF),
            pltpu.VMEM((N, B, B), BF),
            pltpu.VMEM((NC, B, N), BF),
            pltpu.VMEM((N, NC, B), BF),
            pltpu.VMEM((SHARE, NCG), F32),
            pltpu.VMEM((SHARE, NCG), BF),
            pltpu.VMEM((SHARE, NCG), BF),
            pltpu.VMEM((NCG, GRP * NC), BF),
            pltpu.VMEM((NC, NCG), BF),
            pltpu.VMEM((GRP, 8, 128), jnp.int32),
            pltpu.VMEM(packed, BF),
            pltpu.VMEM((2, *packed), BF),
            pltpu.VMEM((N * PITCH, 128), F32),
            pltpu.VMEM((N * PITCH, 128), F32),
            pltpu.VMEM(packed, BF),
            pltpu.VMEM(packed, BF),
            pltpu.VMEM(packed, BF),
            pltpu.VMEM((N, R, B), BF),
            pltpu.VMEM((N, R, B), F32),
            pltpu.VMEM((GRP, R, SHARE), F32),
            pltpu.VMEM((GRP, R, SHARE), F32),
            pltpu.VMEM((R, SHARE), F32),
            pltpu.VMEM((SUB, R, SHARE), F32),
            pltpu.VMEM((GRP, R, 128), F32),
            pltpu.VMEM((GRP, R, 128), F32),
            pltpu.VMEM((8, 128), jnp.int32),
            pltpu.VMEM((N, N), F32),
            pltpu.VMEM((N, N), BF),
            pltpu.VMEM((N, R, B), BF),
            pltpu.VMEM((N, R, B), F32),
            pltpu.SemaphoreType.DMA((2,)),
            pltpu.SemaphoreType.REGULAR,
            pltpu.SemaphoreType.DMA((16,)),
            pltpu.SemaphoreType.DMA((16,)),
            pltpu.SemaphoreType.DMA((8,)),
            pltpu.SemaphoreType.DMA((8,)),
            pltpu.SemaphoreType.DMA((8,)),
            pltpu.SemaphoreType.DMA((8,)),
        ],
        name="assemble_all",
        compiler_params=pltpu.CompilerParams(
            collective_id=0, has_side_effects=True, vmem_limit_bytes=61 << 20
        ),
    )(
        res_inner,
        jnp.transpose(res_face, slots_last),
        inner_inv,
        jnp.transpose(face_coupling, slots_last),
        jnp.transpose(face_inv, slots_last),
        jnp.transpose(coarse_basis, slots_last),
        coarse_inv,
        coarse_map,
        recv_index,
        sharers,
        face_elem,
    )
    inner_out, face_out = pl.pallas_call(
        extend_kernel,
        out_shape=(jax.ShapeDtypeStruct((E, R, B), BF), jax.ShapeDtypeStruct((R, B, N), BF)),
        in_specs=[sm, hbm, hbm, hbm, hbm],
        out_specs=(vm, vm),
        scratch_shapes=[
            pltpu.VMEM((N, R, B), BF),
            pltpu.VMEM((N, R, B), F32),
            pltpu.VMEM((E, R, B), BF),
            pltpu.VMEM((E, R, B), F32),
            pltpu.VMEM((E, B, B), BF),
            pltpu.SemaphoreType.DMA((4,)),
        ],
        name="extend",
        compiler_params=pltpu.CompilerParams(vmem_limit_bytes=61 << 20),
    )(face_elem, rows, terms, res_inner, inner_inv)
    return inner_out, jnp.transpose(face_out, (2, 0, 1))


def solution(mesh):
    split = P(("sub", "grp"), None, None)
    table = P(("sub", "grp"), None)
    return jax.shard_map(
        body,
        mesh=mesh,
        in_specs=(
            split, split, split, split, table, split, split, table, P("grp", None), table, table,
        ),
        out_specs=(split, split),
        check_vma=False,
    )
```

```python
import jax
import jax.numpy as jnp
from jax import lax
from jax.experimental import pallas as pl
from jax.experimental.pallas import tpu as pltpu
from jax.sharding import PartitionSpec as P

MESH = pl.DeviceIdType.MESH
N = 128
E = 64
R = 16
B = 144
NC = 64
NCG = 2048
GRP = 8
SUB = 16
SHARE = NCG // GRP
ROWS = 18
PITCH = 24
BF = jnp.bfloat16
F32 = jnp.float32


def place(t):
    return (t // GRP, t % GRP)


def remote(src, dst, device, s, r):
    return pltpu.make_async_remote_copy(
        src_ref=src, dst_ref=dst, send_sem=s, recv_sem=r, device_id=device, device_id_type=MESH
    )


def put(out, t, rows):
    out[t] = rows.reshape(ROWS // 2, 2, 128).astype(BF)


def get(ref, t):
    return ref[t].reshape(ROWS, 128).astype(F32)


def pack(out, t, value):
    row = lax.broadcasted_iota(jnp.int32, (R, 128), 0)
    lane = lax.broadcasted_iota(jnp.int32, (R, 128), 1)
    tail = jnp.concatenate([value[:, 128:B], jnp.zeros((R, 112), F32)], axis=1)
    for shift in (16, 32, 64):
        tail = tail + pltpu.roll(tail, shift, 1)
    tail = jnp.where((row + lane // 16) % 8 == 0, tail, 0.0)
    tail = jnp.sum(tail.reshape(2, 8, 128), axis=1)
    put(out, t, jnp.concatenate([value[:, 0:128], tail], axis=0))


def unpack(ref, t):
    packed = get(ref, t)
    tail = jnp.broadcast_to(packed[R:ROWS, None, :], (2, 8, 128)).reshape(R, 128)
    tail = pltpu.roll(tail, 0, 1, stride=16, stride_axis=0)
    return jnp.concatenate([packed[0:R], tail[:, 0:16]], axis=1)


def pieces(x):
    high = x.astype(BF)
    rest = x - high.astype(F32)
    mid = rest.astype(BF)
    low = (rest - mid.astype(F32)).astype(BF)
    return jnp.concatenate([high, mid, low], axis=0)


def gather3(x):
    return x[0:R] + x[R : 2 * R] + x[2 * R : 3 * R]


def rows_times(a, b):
    return lax.dot_general(a, b, (((1,), (1,)), ((), ())), preferred_element_type=F32)


def main_kernel(
    res_inner_h, res_face_h, inner_inv_h, coupling_h, face_inv_h, basis_h, coarse_inv_h,
    map_row_own, index_row, sharers, elem,
    rows_h, terms_h,
    res_inner, inner_inv, inner_w, res_face, face_rows, stage, coupling, face_inv, basis_stage, basis,
    coarse_inv, coarse_high, coarse_low, pick, own_pick, maps,
    sent, received, wide, wide2, back, gathered, gathered2, restricted, local,
    part, part_in, share, share_in, chosen, chosen_in, map_block, weight, contrast,
    rows_out, terms_out, out_sems, entered, piece_sems, batch_sems, load_sems, send_sems, recv_sems, own_sems,
):
    sub = lax.axis_index("sub")
    grp = lax.axis_index("grp")
    me = sub * GRP + grp
    barrier = pltpu.get_barrier_semaphore()

    def load(src, dst, k):
        return pltpu.make_async_copy(src, dst, load_sems.at[k])

    load(res_inner_h, res_inner, 0).start()

    def piece(src, dst, q, k):
        rows = pl.ds(pl.multiple_of(q * 16, 16), 16)
        return pltpu.make_async_copy(src.at[rows], dst.at[rows], piece_sems.at[k + q])

    def inverse_piece(q):
        return piece(inner_inv_h, inner_inv, q, 0)

    def coupling_piece(q):
        return piece(coupling_h, stage, q, 4)

    for q in range(9):
        coupling_piece(q).start()
    for q in range(4):
        inverse_piece(q).start()
    load(res_face_h, res_face, 3).start()

    def signal(semaphore, device):
        pl.semaphore_signal(semaphore, inc=1, device_id=device, device_id_type=MESH)

    def each(first, last, f, unroll=1):
        def one(i, c):
            f(i)
            return c

        lax.fori_loop(first, last, one, 0, unroll=unroll)

    each(1, GRP, lambda i: signal(barrier, (sub, lax.rem(grp + i, GRP))))
    each(1, SUB, lambda i: signal(barrier, (lax.rem(sub + i, SUB), grp)))

    def tall(row):
        return jnp.broadcast_to(row, (N, N)).T

    counts = sharers[...]
    weight[...] = tall(jnp.where(counts > 0, 1.0 / jnp.maximum(counts, 1).astype(F32), 0.0))
    map_own = jnp.concatenate([map_row_own[...], jnp.zeros((1, 128 - NC), jnp.int32)], axis=1)
    map_block[...] = jnp.broadcast_to(map_own, (8, 128))
    index = index_row[...].astype(F32)
    contrast[...] = jnp.where((index == tall(index)) & (index < 32.0), 1.0, 0.0).astype(BF)

    def turn(src, dst, q):
        part_rows = src[pl.ds(pl.multiple_of(q * 16, 16), 16)]
        part_rows = jnp.swapaxes(jnp.swapaxes(part_rows, 1, 2), 0, 1)
        dst[:, pl.ds(pl.multiple_of(q * 16, 16), 16), :] = part_rows

    def turns(src, dst, first, last):
        def one(q, c):
            turn(src, dst, q)
            return c

        lax.fori_loop(first, last, one, 0)

    def coupling_turn(q):
        coupling_piece(q).wait()
        turn(stage, coupling, q)

    each(0, 9, coupling_turn)
    load(face_inv_h, stage, 6).start()
    pl.semaphore_wait(barrier, GRP + SUB - 2)
    each(1, SUB, lambda i: signal(entered, (lax.rem(sub + i, SUB), grp)))

    def inner(e):
        inner_w[e] = rows_times(res_inner[e], inner_inv[e]).astype(BF)

    load(res_inner_h, res_inner, 0).wait()

    def inners(q):
        inverse_piece(q).wait()
        for e in range(16):
            inner(16 * q + e)

    each(0, 4, inners)
    load(basis_h, basis_stage, 4).start()
    load(coarse_inv_h, coarse_inv, 5).start()
    load(res_face_h, res_face, 3).wait()
    turns(res_face, face_rows, 0, 1)
    pl.semaphore_wait(entered, SUB - 1)

    def map_copy(i):
        return remote(map_block, maps.at[grp], (sub, lax.rem(grp + i, GRP)), send_sems.at[0], recv_sems.at[0])

    own_map = pltpu.make_async_copy(map_block, maps.at[grp], own_sems.at[0])
    own_map.start()
    each(1, GRP, lambda i: map_copy(i).start())

    def quad(i):
        return lax.rem(me // 4 + i, N // 4) * 4

    def exchange(source, target, k, fill, arrived, size):
        def give(t, j):
            remote(source.at[t], target.at[me], place(t), send_sems.at[k], arrived(j // 16)).start()

        def batch(q):
            for i in range(size // 4):
                fill(quad(q * (size // 4) + i))

        def pass_on(j):
            give(quad(j // 4) + lax.rem(me + j, 4), j)

        batch(0)
        own = pltpu.make_async_copy(source.at[me], target.at[me], own_sems.at[k])
        own.start()
        each(1, size, pass_on)

        def more(q):
            batch(q)
            each(size * q, size * q + size, pass_on)

        each(1, N // size, more)
        return own

    def all_at_once(k):
        return lambda q: recv_sems.at[k]

    def in_batches(c):
        return lambda q: batch_sems.at[c * 8 + q]

    def sent_all(source, k):
        rest = source.at[pl.ds(0, N - 1)]
        remote(rest, rest, (sub, grp), send_sems.at[k], recv_sems.at[k]).wait_send()

    def arrive(source, target, k, own):
        own.wait()
        rest = target.at[pl.ds(0, N - 1)]
        remote(rest, rest, (sub, grp), send_sems.at[k], recv_sems.at[k]).wait_recv()
        sent_all(source, k)

    def arrive_in_batches(source, target, k, own, arrived, use, carry):
        def wait(q, count):
            some = target.at[pl.ds(0, count)]
            remote(some, some, (sub, grp), send_sems.at[k], arrived(q)).wait_recv()

        def use_batch(q, carry):
            return use([quad(N // 4 - 4 * q - i) for i in range(4)], carry)

        def next_batch(q, carry):
            wait(q, 16)
            return use_batch(q, carry)

        own.wait()
        wait(0, 15)
        carry = lax.fori_loop(1, N // 16, next_batch, use_batch(0, carry))
        sent_all(source, k)
        return carry

    def scaled(t, value):
        scale = jnp.broadcast_to(weight[pl.ds(t, 1), :], (R, 128))
        return jnp.concatenate([scale, scale[:, 0:16]], axis=1) * value

    def condense(base):
        for t in [base + k for k in range(4)]:
            product = rows_times(inner_w[elem[0, t]], coupling[t])
            pack(sent, t, scaled(t, face_rows[t].astype(F32) - product))

    own = exchange(sent, received.at[0], 1, condense, all_at_once(1), 32)
    load(face_inv_h, stage, 6).wait()
    load(basis_h, basis_stage, 4).wait()
    turns(basis_stage, basis, 0, 4)
    turns(stage, face_inv, 0, 5)
    arrive(sent, received.at[0], 1, own)

    same = contrast[...]

    def owner_sum(source):
        def widen(s):
            wide[pl.ds(pl.multiple_of(s * PITCH, 8), ROWS)] = get(source, s)

        each(0, N, widen, 8)
        for k in range(ROWS):
            rows = wide[pl.ds(k, N, stride=PITCH), :].astype(BF)
            wide2[pl.ds(k, N, stride=PITCH), :] = jnp.dot(same, rows, preferred_element_type=F32)

    def narrow(target):
        def one(base):
            for t in [base + k for k in range(4)]:
                put(target, t, wide2[pl.ds(pl.multiple_of(t * PITCH, 8), ROWS)])

        return one

    owner_sum(received.at[0])
    own = exchange(back, gathered, 2, narrow(back), in_batches(0), 16)

    turns(stage, face_inv, 5, 9)
    load(coarse_inv_h, coarse_inv, 5).wait()

    def split(q):
        rows = pl.ds(pl.multiple_of(q * 16, 16), 16)
        high = coarse_inv[rows, :].astype(BF)
        coarse_high[rows, :] = high
        coarse_low[rows, :] = (coarse_inv[rows, :] - high.astype(F32)).astype(BF)

    each(0, SHARE // 16, split)
    own_map.wait()
    seven = pl.ds(0, GRP - 1)
    remote(maps.at[seven], maps.at[seven], (sub, grp), send_sems.at[0], recv_sems.at[0]).wait()
    map_row = jnp.concatenate([maps[g, 0:1, 0:NC] for g in range(GRP)], axis=1)

    def mark(q):
        at = lax.broadcasted_iota(jnp.int32, (128, GRP * NC), 0) + q * 128
        pick[pl.ds(pl.multiple_of(q * 128, 128), 128), :] = jnp.where(map_row == at, 1.0, 0.0).astype(BF)

    each(0, NCG // 128, mark)
    map_tall = tall(map_own.astype(F32))[0:NC]
    for q in range(NCG // 128):
        at = (lax.broadcasted_iota(jnp.int32, (NC, 128), 1) + q * 128).astype(F32)
        own_pick[:, q * 128 : (q + 1) * 128] = jnp.where(map_tall == at, 1.0, 0.0).astype(BF)

    def basis4(q):
        return basis[pl.ds(pl.multiple_of(q * 4, 4), 4)].reshape(4 * NC, B)

    def project(bases, total):
        for base in bases:
            rows = []
            for t in [base + k for k in range(4)]:
                rows.append(scaled(t, unpack(gathered, t)).astype(BF))
                restricted[t] = rows[-1]
            total = total + rows_times(jnp.concatenate(rows, axis=0), basis4(base // 4))
        return total

    crossed = arrive_in_batches(
        back, gathered, 2, own, in_batches(0), project, jnp.zeros((4 * R, 4 * NC), F32)
    )
    local_coarse = sum(crossed[k * R : (k + 1) * R, k * NC : (k + 1) * NC] for k in range(4))

    partial = gather3(jnp.dot(pieces(local_coarse), own_pick[...], preferred_element_type=F32))
    for g in range(GRP):
        part[g] = partial[:, g * SHARE : (g + 1) * SHARE]

    own = pltpu.make_async_copy(part.at[grp], part_in.at[grp], own_sems.at[3])
    own.start()

    def ring_send(source, target, k):
        def one(i):
            t = lax.rem(grp + i, GRP)
            remote(source.at[t], target.at[grp], (sub, t), send_sems.at[k], recv_sems.at[k]).start()

        each(1, GRP, one)

    def ring_wait(source, target, k):
        remote(source.at[seven], target.at[seven], (sub, grp), send_sems.at[k], recv_sems.at[k]).wait()

    def solve_local(t):
        local[t] = rows_times(restricted[t], face_inv[t])

    ring_send(part, part_in, 3)
    each(0, 64, solve_local, 32)
    own.wait()
    ring_wait(part, part_in, 3)
    share[...] = jnp.sum(part_in[...], axis=0)
    own = pltpu.make_async_copy(share, share_in.at[sub], own_sems.at[4])
    own.start()

    def share_copy(i):
        t = lax.rem(sub + i, SUB)
        remote(share, share_in.at[sub], (t, grp), send_sems.at[4], recv_sems.at[4]).start()

    each(1, SUB, share_copy)
    each(64, N, solve_local, 32)
    own.wait()
    fifteen = pl.ds(0, SUB - 1)
    remote(share_in.at[fifteen], share_in.at[fifteen], (sub, grp), send_sems.at[4], recv_sems.at[4]).wait()
    total = pieces(jnp.sum(share_in[...], axis=0))
    term = gather3(
        jnp.dot(total, coarse_high[...], preferred_element_type=F32)
        + jnp.dot(total, coarse_low[...], preferred_element_type=F32)
    )
    picked = gather3(jnp.dot(pieces(term), pick[...], preferred_element_type=F32))
    for g in range(GRP):
        chosen[g, :, 0:NC] = picked[:, g * NC : (g + 1) * NC]
        chosen[g, :, NC:128] = jnp.zeros((R, 128 - NC), F32)
    own = pltpu.make_async_copy(chosen.at[grp], chosen_in.at[grp], own_sems.at[5])
    own.start()
    ring_send(chosen, chosen_in, 5)
    own.wait()
    ring_wait(chosen, chosen_in, 5)
    mine = jnp.sum(chosen_in[...], axis=0)[:, 0:NC]
    row = lax.broadcasted_iota(jnp.int32, (4 * R, 4 * NC), 0) // R
    lane = lax.broadcasted_iota(jnp.int32, (4 * R, 4 * NC), 1) // NC
    mine4 = jnp.concatenate([jnp.concatenate([mine] * 4, axis=1)] * 4, axis=0)
    mine4 = jnp.where(row == lane, mine4, 0.0).astype(BF)

    def correct(base):
        coarse = jnp.dot(mine4, basis4(base // 4), preferred_element_type=F32)
        for k in range(4):
            pack(sent, base + k, scaled(base + k, local[base + k] + coarse[k * R : (k + 1) * R]))

    own = exchange(sent, received.at[1], 6, correct, all_at_once(6), 32)
    arrive(sent, received.at[1], 6, own)
    owner_sum(received.at[1])
    own = exchange(back, gathered2, 7, narrow(back), in_batches(1), 16)

    def extend(bases, carry):
        for base in bases:
            for t in [base + k for k in range(4)]:
                rows = unpack(gathered2, t).astype(BF)
                rows_out[t] = rows
                terms_out[t] = jnp.dot(rows, coupling[t], preferred_element_type=F32)
        for base in bases:
            four = pl.ds(base, 4)
            pltpu.make_async_copy(rows_out.at[four], rows_h.at[four], out_sems.at[0]).start()
            pltpu.make_async_copy(terms_out.at[four], terms_h.at[four], out_sems.at[1]).start()
        return carry

    arrive_in_batches(back, gathered2, 7, own, in_batches(1), extend, 0)
    pltpu.make_async_copy(rows_out, rows_h, out_sems.at[0]).wait()
    pltpu.make_async_copy(terms_out, terms_h, out_sems.at[1]).wait()


def extend_kernel(
    elem, rows_h, terms_h, res_inner_h, inner_inv_h, inner_out, face_out,
    rows, terms, res_inner, total, inner_inv, sems,
):
    pairs = ((res_inner_h, res_inner), (terms_h, terms), (rows_h, rows), (inner_inv_h, inner_inv))
    loads = [pltpu.make_async_copy(src, dst, sems.at[k]) for k, (src, dst) in enumerate(pairs)]
    for one in loads:
        one.start()
    loads[0].wait()
    total[...] = res_inner[...].astype(F32)
    loads[1].wait()

    def add(t, c):
        e = elem[0, t]
        total[e] = total[e] - terms[t]
        return c

    lax.fori_loop(0, N, add, 0, unroll=8)
    loads[2].wait()
    face_out[...] = jnp.swapaxes(jnp.swapaxes(rows[...], 0, 1), 1, 2)
    loads[3].wait()

    def inner(e, c):
        inner_out[e] = rows_times(total[e].astype(BF), inner_inv[e]).astype(BF)
        return c

    lax.fori_loop(0, E, inner, 0, unroll=32)


def body(
    res_inner, res_face, inner_inv, face_coupling, face_elem, face_inv, coarse_basis, coarse_map, coarse_inv,
    recv_index, sharers,
):
    vm = pl.BlockSpec(memory_space=pltpu.VMEM)
    hbm = pl.BlockSpec(memory_space=pl.ANY)
    sm = pl.BlockSpec(memory_space=pltpu.SMEM)
    slots_last = (1, 2, 0)
    packed = (N, ROWS // 2, 2, 128)
    rows, terms = pl.pallas_call(
        main_kernel,
        out_shape=(jax.ShapeDtypeStruct((N, R, B), BF), jax.ShapeDtypeStruct((N, R, B), F32)),
        in_specs=[hbm] * 7 + [vm] * 3 + [sm],
        out_specs=(hbm, hbm),
        scratch_shapes=[
            pltpu.VMEM((E, R, B), BF),
            pltpu.VMEM((E, B, B), BF),
            pltpu.VMEM((E, R, B), BF),
            pltpu.VMEM((R, B, N), BF),
            pltpu.VMEM((N, R, B), BF),
            pltpu.VMEM((B, B, N), BF),
            pltpu.VMEM((N, B, B), BF),
            pltpu.VMEM((N, B, B), BF),
            pltpu.VMEM((NC, B, N), BF),
            pltpu.VMEM((N, NC, B), BF),
            pltpu.VMEM((SHARE, NCG), F32),
            pltpu.VMEM((SHARE, NCG), BF),
            pltpu.VMEM((SHARE, NCG), BF),
            pltpu.VMEM((NCG, GRP * NC), BF),
            pltpu.VMEM((NC, NCG), BF),
            pltpu.VMEM((GRP, 8, 128), jnp.int32),
            pltpu.VMEM(packed, BF),
            pltpu.VMEM((2, *packed), BF),
            pltpu.VMEM((N * PITCH, 128), F32),
            pltpu.VMEM((N * PITCH, 128), F32),
            pltpu.VMEM(packed, BF),
            pltpu.VMEM(packed, BF),
            pltpu.VMEM(packed, BF),
            pltpu.VMEM((N, R, B), BF),
            pltpu.VMEM((N, R, B), F32),
            pltpu.VMEM((GRP, R, SHARE), F32),
            pltpu.VMEM((GRP, R, SHARE), F32),
            pltpu.VMEM((R, SHARE), F32),
            pltpu.VMEM((SUB, R, SHARE), F32),
            pltpu.VMEM((GRP, R, 128), F32),
            pltpu.VMEM((GRP, R, 128), F32),
            pltpu.VMEM((8, 128), jnp.int32),
            pltpu.VMEM((N, N), F32),
            pltpu.VMEM((N, N), BF),
            pltpu.VMEM((N, R, B), BF),
            pltpu.VMEM((N, R, B), F32),
            pltpu.SemaphoreType.DMA((2,)),
            pltpu.SemaphoreType.REGULAR,
            pltpu.SemaphoreType.DMA((16,)),
            pltpu.SemaphoreType.DMA((16,)),
            pltpu.SemaphoreType.DMA((8,)),
            pltpu.SemaphoreType.DMA((8,)),
            pltpu.SemaphoreType.DMA((8,)),
            pltpu.SemaphoreType.DMA((8,)),
        ],
        name="assemble_all",
        compiler_params=pltpu.CompilerParams(
            collective_id=0, has_side_effects=True, vmem_limit_bytes=61 << 20
        ),
    )(
        res_inner,
        jnp.transpose(res_face, slots_last),
        inner_inv,
        jnp.transpose(face_coupling, slots_last),
        jnp.transpose(face_inv, slots_last),
        jnp.transpose(coarse_basis, slots_last),
        coarse_inv,
        coarse_map,
        recv_index,
        sharers,
        face_elem,
    )
    inner_out, face_out = pl.pallas_call(
        extend_kernel,
        out_shape=(jax.ShapeDtypeStruct((E, R, B), BF), jax.ShapeDtypeStruct((R, B, N), BF)),
        in_specs=[sm, hbm, hbm, hbm, hbm],
        out_specs=(vm, vm),
        scratch_shapes=[
            pltpu.VMEM((N, R, B), BF),
            pltpu.VMEM((N, R, B), F32),
            pltpu.VMEM((E, R, B), BF),
            pltpu.VMEM((E, R, B), F32),
            pltpu.VMEM((E, B, B), BF),
            pltpu.SemaphoreType.DMA((4,)),
        ],
        name="extend",
        compiler_params=pltpu.CompilerParams(vmem_limit_bytes=61 << 20),
    )(face_elem, rows, terms, res_inner, inner_inv)
    return inner_out, jnp.transpose(face_out, (2, 0, 1))


def solution(mesh):
    split = P(("sub", "grp"), None, None)
    table = P(("sub", "grp"), None)
    return jax.shard_map(
        body,
        mesh=mesh,
        in_specs=(
            split, split, split, split, table, split, split, table, P("grp", None), table, table,
        ),
        out_specs=(split, split),
        check_vma=False,
    )
```
